256 devices in a mesh: layer: 64 (over z, y, x_lo), row: 2 (over x_hi), col: 2 (over core).
Axes of the slice: x: 4 (x_hi: 2, x_lo: 2; x = x_hi * 2 + x_lo), y: 4, z: 8, core: 2. Of those that a mesh axis runs over, the one named last changes fastest.
Arguments:
- markov: bfloat16 [16384, 16384], P('row', ('layer', 'col')), may hold values from 0.049804688 to 1
- markov_tiles: int32 [256, 256], P('row', ('layer', 'col')), may hold values from 0 to 1, as said below
- slab: bfloat16 [16384, 2048], P(('layer', 'row'), 'col'), may hold values from 0.049804688 to 1
- slab_tiles: int32 [256, 32], P(('layer', 'row'), 'col'), may hold values from 0 to 1, as said below
Outputs:
- inflated: float32 [16384, 2048], P(('row', 'layer'), 'col')
The draws below stay inside these ranges and needn't reach their ends.
Inputs may be any that keep to these rules, and one draw needn't show every extreme that they name: `markov_tiles`: every diagonal tile of the network matrix is present. `slab_tiles`: tile (c, c) of the slab is present for every slab tile column c.
All inputs are finite; a program needn't handle non-finite values.
Results may differ from the reference program's by a relative error of at most 0.0003.
Values may be sent and summed in bfloat16 or wider, within the bound.
No kernel may reach another device: no remote copies, remote signals or barrier semaphores. Data moves between devices by JAX's collectives and lax.ppermute only.
A program may use at most 128 MiB of HBM per device.

```python
import math
import jax
import jax.numpy as jnp

TILE = 64
TILES = 256
SLAB_TILES = 32
ORDER = 16384
SLAB = 2048


def draw_markov_tiles(key, part):
    key = jax.random.fold_in(key, 11)
    picks = jax.random.randint(key, (TILES, TILES), 0, 20)
    diagonal = jnp.arange(TILES)[:, None] == jnp.arange(TILES)[None, :]
    return jnp.where((picks < 1) | diagonal, 1, 0).astype(jnp.int32)


def draw_slab_tiles(key, part):
    key = jax.random.fold_in(key, 23)
    picks = jax.random.randint(key, (TILES, SLAB_TILES), 0, 20)
    diagonal = jnp.arange(TILES)[:, None] == jnp.arange(SLAB_TILES)[None, :]
    return jnp.where((picks < 5) | diagonal, 1, 0).astype(jnp.int32)


def steps_of(key, shape, shards, least, high):
    factor_of = 1.0
    for dim, shards_of in shards:
        heights = jax.random.uniform(jax.random.fold_in(jax.random.fold_in(key, 6), dim), (shards_of,), jnp.float32, least / len(shards), high / len(shards))
        factor_of = factor_of * jnp.repeat(jnp.exp(heights), shape[dim] // shards_of).reshape((-1,) + (1,) * (len(shape) - 1 - dim))
    return factor_of


def setup_inputs(seed: int = 0) -> dict:
    streams_of = jax.random.split(jax.random.key(seed), 5)
    return {
        "markov": jnp.clip(jnp.exp(math.log(1.0) - 2.9996462 * jax.random.uniform(streams_of[0], (ORDER, ORDER), jnp.float32) ** steps_of(streams_of[0], (ORDER, ORDER), ((0, 2), (1, 128)), -0.2, 0.2)), 0.049804688, 1.0).astype(jnp.bfloat16),
        "markov_tiles": draw_markov_tiles(jax.random.fold_in(streams_of[4], 71), 0),
        "slab": jnp.clip(jnp.exp(math.log(1.0) - 2.9996462 * jax.random.uniform(streams_of[2], (ORDER, SLAB), jnp.float32) ** steps_of(streams_of[2], (ORDER, SLAB), ((0, 128), (1, 2)), -0.2, 0.2)), 0.049804688, 1.0).astype(jnp.bfloat16),
        "slab_tiles": draw_slab_tiles(jax.random.fold_in(streams_of[4], 71), 0),
    }


def widen(pattern, tile):
    rows, cols = pattern.shape
    ones = pattern.astype(jnp.bfloat16)
    return jnp.broadcast_to(ones[:, None, :, None], (rows, tile, cols, tile)).reshape(rows * tile, cols * tile)


def reference(markov, markov_tiles, slab, slab_tiles):
    left = markov * widen(markov_tiles, TILE)
    right = slab * widen(slab_tiles, TILE)
    expanded = jnp.dot(left, right, preferred_element_type=jnp.float32)
    squared = expanded * expanded
    column_mean = jnp.sum(squared, axis=0) / ORDER
    return squared / (column_mean[None, :] + 1e-6)
```

```python
import functools

import jax
import jax.numpy as jnp
from jax import lax
from jax.experimental import pallas as pl
from jax.experimental.pallas import tpu as pltpu
from jax.sharding import Mesh
from jax.sharding import PartitionSpec as P

NZ, NY, NX = 8, 4, 2
TILE = 64
ALL = ("z", "y", "xl", "xh")
LOW = -2.75
STEP = 13.8 / 65534.0


def lanes(rows):
    return lax.broadcasted_iota(jnp.int32, (rows, 128), 1) < TILE


def mask_kernel(tiles, x_ref, o_ref):
    rows, cols = x_ref.shape
    half = lanes(TILE)
    base = pl.program_id(0) * (rows // TILE)
    for i in range(rows // TILE):
        for g in range(cols // 128):
            keep = jnp.where(half, tiles[base + i, 2 * g], tiles[base + i, 2 * g + 1])
            at = (pl.ds(i * TILE, TILE), pl.ds(g * 128, 128))
            x = x_ref[at].astype(jnp.float32)
            o_ref[at] = jnp.where(keep != 0, x, 0.0).astype(o_ref.dtype)


def masked(x, tiles, block):
    return pl.pallas_call(
        mask_kernel,
        grid=(x.shape[0] // block,),
        in_specs=[
            pl.BlockSpec(memory_space=pltpu.SMEM),
            pl.BlockSpec((block, x.shape[1]), lambda i: (i, 0)),
        ],
        out_specs=pl.BlockSpec((block, x.shape[1]), lambda i: (i, 0)),
        out_shape=jax.ShapeDtypeStruct(x.shape, x.dtype),
        name="mask",
    )(tiles, x)


def encode(p):
    code = jnp.round((jnp.log2(jnp.maximum(p, 0.15)) - LOW) * (1.0 / STEP)) - 32767.0
    return jnp.where(p > 0.0, code, -32768.0).astype(jnp.int32).astype(jnp.int16)


def decode(q):
    f = q.astype(jnp.int32).astype(jnp.float32)
    return jnp.where(f > -32768.0, jnp.exp2((f + 32767.0) * STEP + LOW), 0.0)


def product_kernel(own_ref, other_ref, *refs):
    slabs, (out_ref, left, right, sems) = refs[:-4], refs[-4:]
    z = lax.axis_index("z")
    same = lax.axis_index("xh") == lax.axis_index("core")
    copies = []

    def copy(src, dst):
        copies.append(pltpu.make_async_copy(src, dst, sems.at[len(copies)]))
        copies[-1].start()

    for k in range(NZ):
        copy(own_ref.at[k], left.at[:, pl.ds(256 * k, 128)])
        copy(other_ref.at[k], left.at[:, pl.ds(256 * k + 128, 128)])
    for mine in (True, False):
        slot = jnp.where(same, 0, 1) if mine else jnp.where(same, 1, 0)
        for i, (d, top) in enumerate(OFFSETS):
            ref = slabs[i if mine else i + len(OFFSETS)]
            row = lax.rem(z + d, NZ) * 256 + slot * 128 + top
            copy(ref, right.at[pl.ds(pl.multiple_of(row, 64), ref.shape[0]), :])
    for c in copies:
        c.wait()
    rows = 256
    for m in range(1024 // rows):
        p = jnp.dot(left[pl.ds(m * rows, rows), :], right[...], preferred_element_type=jnp.float32)
        q = encode(p)
        for i in range(rows // 128):
            out_ref[m * rows // 128 + i] = q[i * 128 : (i + 1) * 128]


OFFSETS = ((0, 0), (7, 0), (1, 0), (6, 0), (2, 0), (5, 0), (3, 0), (4, 0), (4, 64))


def product(own, other, slabs):
    n = 16 + len(slabs)
    return pl.pallas_call(
        product_kernel,
        in_specs=[pl.BlockSpec(memory_space=pl.ANY)] * (2 + len(slabs)),
        out_specs=pl.BlockSpec(memory_space=pltpu.VMEM),
        out_shape=jax.ShapeDtypeStruct((8, 128, 1024), jnp.int16),
        scratch_shapes=[
            pltpu.VMEM((1024, 2048), jnp.bfloat16),
            pltpu.VMEM((2048, 1024), jnp.bfloat16),
            pltpu.SemaphoreType.DMA((n,)),
        ],
        compiler_params=pltpu.CompilerParams(vmem_limit_bytes=40 * 2**20),
        cost_estimate=pl.CostEstimate(flops=2 * 1024 * 2048 * 1024, bytes_accessed=10 * 2**20, transcendentals=2**20),
        name="product",
    )(own, other, *slabs)


def square_kernel(q_ref, s_ref, sum_ref):
    total = decode(q_ref[0])
    for i in range(1, 8):
        total = total + decode(q_ref[i])
    s = total * total
    s_ref[...] = s
    sum_ref[...] = jnp.sum(s, axis=0, keepdims=True)


def squares(q):
    return pl.pallas_call(
        square_kernel,
        grid=(4,),
        in_specs=[pl.BlockSpec((8, 128, 256), lambda i: (0, 0, i))],
        out_specs=[pl.BlockSpec((128, 256), lambda i: (0, i)), pl.BlockSpec((1, 256), lambda i: (0, i))],
        out_shape=[jax.ShapeDtypeStruct((128, 1024), jnp.float32), jax.ShapeDtypeStruct((1, 1024), jnp.float32)],
        name="squares",
    )(q)


def gather_slab(block):
    up = functools.partial(lax.ppermute, axis_name="z", perm=[(i, (i + 1) % NZ) for i in range(NZ)])
    down = functools.partial(lax.ppermute, axis_name="z", perm=[(i, (i - 1) % NZ) for i in range(NZ)])
    p1, n1 = up(block), down(block)
    p2, n2 = up(p1), down(n1)
    p3, n3 = up(p2), down(n2)
    p4, n4 = up(p3[:64]), down(n3[64:])
    mine = [block, p1, n1, p2, n2, p3, n3, p4, n4]
    return mine + [lax.ppermute(b, "xh", [(0, 1), (1, 0)]) for b in mine]


def per_device(markov, markov_tiles, slab, slab_tiles):
    right = gather_slab(masked(slab, slab_tiles, 128))
    left = masked(markov, markov_tiles, 1024).reshape(NZ, 1024, 128)
    own = lax.all_to_all(left, "z", 0, 0, tiled=True)
    other = lax.ppermute(own, "core", [(0, 1), (1, 0)])
    codes = product(own, other, right)
    codes = lax.all_to_all(codes, ("y", "xl"), 0, 0, tiled=True)
    squared, sums = squares(codes)
    sums = lax.all_to_all(jnp.broadcast_to(sums[None], (128, 1, 1024)), ALL, 0, 0, tiled=True)
    column_mean = jnp.sum(sums, axis=(0, 1)) / 16384.0
    return squared / (column_mean[None, :] + 1e-06)


def solution(mesh):
    fine = Mesh(mesh.devices.reshape(NZ, NY, NX, 2, 2), ("z", "y", "xl", "xh", "core"))
    layer = ("z", "y", "xl")
    in_specs = (
        P("xh", layer + ("core",)),
        P("xh", layer + ("core",)),
        P(layer + ("xh",), "core"),
        P(layer + ("xh",), "core"),
    )
    return jax.shard_map(
        per_device, mesh=fine, in_specs=in_specs, out_specs=P(("xh",) + layer, "core"), check_vma=False
    )
```

```python
import functools

import jax
import jax.numpy as jnp
from jax import lax
from jax.experimental import pallas as pl
from jax.experimental.pallas import tpu as pltpu
from jax.sharding import Mesh
from jax.sharding import PartitionSpec as P

NZ, NY, NX = 8, 4, 2
TILE = 64
CAP = 12
ALL = ("z", "y", "xl", "xh")
LOW = -2.75
STEP = 13.8 / 65534.0


def lanes(rows):
    return lax.broadcasted_iota(jnp.int32, (rows, 128), 1) < TILE


def mask_kernel(tiles, x_ref, o_ref):
    rows, cols = x_ref.shape
    half = lanes(TILE)
    base = pl.program_id(0) * (rows // TILE)
    for i in range(rows // TILE):
        for g in range(cols // 128):
            keep = jnp.where(half, tiles[base + i, 2 * g], tiles[base + i, 2 * g + 1])
            at = (pl.ds(i * TILE, TILE), pl.ds(g * 128, 128))
            x = x_ref[at].astype(jnp.float32)
            o_ref[at] = jnp.where(keep != 0, x, 0.0).astype(o_ref.dtype)


def masked(x, tiles, block):
    return pl.pallas_call(
        mask_kernel,
        grid=(x.shape[0] // block,),
        in_specs=[
            pl.BlockSpec(memory_space=pltpu.SMEM),
            pl.BlockSpec((block, x.shape[1]), lambda i: (i, 0)),
        ],
        out_specs=pl.BlockSpec((block, x.shape[1]), lambda i: (i, 0)),
        out_shape=jax.ShapeDtypeStruct(x.shape, x.dtype),
        name="mask",
    )(tiles, x)


def halves(x):
    return jnp.concatenate([x[:, TILE:], x[:, :TILE]], axis=1)


def pack_kernel(tiles, flags_ref, x_ref, o_ref):
    left = (lax.broadcasted_iota(jnp.int32, (32, 128), 1) < TILE).astype(jnp.float32).astype(x_ref.dtype)
    right = 1 - left
    base = pl.program_id(0) * 16
    o_ref[...] = jnp.zeros_like(o_ref)
    slot = 0
    for i in range(16):
        top, bottom = x_ref[pl.ds(i * TILE, 32), :], x_ref[pl.ds(i * TILE + 32, 32), :]
        pair = (top * left + halves(bottom) * right, halves(top) * left + bottom * right)
        for j in range(2):
            o_ref[0, pl.ds(pl.multiple_of(slot * 32, 32), 32), :] = pair[j]
            slot = jnp.minimum(slot + tiles[base + i, j], CAP)
    o_ref[0, pl.ds(CAP * 32, 32), :] = jnp.zeros((32, 128), o_ref.dtype)
    o_ref[0, pl.ds(CAP * 32 + 32, 16), :] = flags_ref[...]


def pack(markov, tiles):
    flags = jnp.pad(tiles.astype(markov.dtype), ((0, 0), (0, 126)))
    return pl.pallas_call(
        pack_kernel,
        grid=(NZ,),
        in_specs=[
            pl.BlockSpec(memory_space=pltpu.SMEM),
            pl.BlockSpec((16, 128), lambda i: (i, 0)),
            pl.BlockSpec((1024, 128), lambda i: (i, 0)),
        ],
        out_specs=pl.BlockSpec((1, CAP * 32 + 48, 128), lambda i: (i, 0, 0)),
        out_shape=jax.ShapeDtypeStruct((NZ, CAP * 32 + 48, 128), markov.dtype),
        name="pack",
    )(tiles, flags, markov)


def unpack_kernel(flags, x_ref, o_ref):
    left = (lax.broadcasted_iota(jnp.int32, (32, 128), 1) < TILE).astype(jnp.float32).astype(x_ref.dtype)
    right = 1 - left
    base = pl.program_id(0) * 32
    slot = 0
    for i in range(16):
        pair = []
        for j in range(2):
            flag = flags[base + 2 * i + j]
            at = jnp.minimum(jnp.where(flag > 0, slot, CAP), CAP)
            pair.append(x_ref[0, pl.ds(pl.multiple_of(at * 32, 32), 32), :])
            slot = slot + flag
        o_ref[0, pl.ds(i * TILE, 32), :] = pair[0] * left + halves(pair[1]) * right
        o_ref[0, pl.ds(i * TILE + 32, 32), :] = halves(pair[0]) * left + pair[1] * right


def unpack(packed, flags):
    return pl.pallas_call(
        unpack_kernel,
        grid=(NZ,),
        in_specs=[
            pl.BlockSpec(memory_space=pltpu.SMEM),
            pl.BlockSpec((1, CAP * 32 + 48, 128), lambda i: (i, 0, 0)),
        ],
        out_specs=pl.BlockSpec((1, 1024, 128), lambda i: (i, 0, 0)),
        out_shape=jax.ShapeDtypeStruct((NZ, 1024, 128), packed.dtype),
        name="unpack",
    )(flags, packed)


def flags_of(packed):
    return packed[:, CAP * 32 + 32 :, :2].astype(jnp.int32).reshape(NZ, 32)


def encode(p):
    code = jnp.round((jnp.log2(jnp.maximum(p, 0.15)) - LOW) * (1.0 / STEP)) - 32767.0
    return jnp.where(p > 0.0, code, -32768.0).astype(jnp.int32).astype(jnp.int16)


def decode(q):
    f = q.astype(jnp.int32).astype(jnp.float32)
    return jnp.where(f > -32768.0, jnp.exp2((f + 32767.0) * STEP + LOW), 0.0)


def product_kernel(own_ref, other_ref, *refs):
    slabs, (out_ref, left, right, sems) = refs[:-4], refs[-4:]
    z = lax.axis_index("z")
    same = lax.axis_index("xh") == lax.axis_index("core")
    copies = []

    def copy(src, dst):
        copies.append(pltpu.make_async_copy(src, dst, sems.at[len(copies)]))
        copies[-1].start()

    for k in range(NZ):
        copy(own_ref.at[k], left.at[:, pl.ds(256 * k, 128)])
        copy(other_ref.at[k], left.at[:, pl.ds(256 * k + 128, 128)])
    for mine in (True, False):
        slot = jnp.where(same, 0, 1) if mine else jnp.where(same, 1, 0)
        for i, (d, top) in enumerate(OFFSETS):
            ref = slabs[i if mine else i + len(OFFSETS)]
            row = lax.rem(z + d, NZ) * 256 + slot * 128 + top
            copy(ref, right.at[pl.ds(pl.multiple_of(row, 64), ref.shape[0]), :])
    for c in copies:
        c.wait()
    rows = 256
    for m in range(1024 // rows):
        p = jnp.dot(left[pl.ds(m * rows, rows), :], right[...], preferred_element_type=jnp.float32)
        q = encode(p)
        for i in range(rows // 128):
            out_ref[m * rows // 128 + i] = q[i * 128 : (i + 1) * 128]


OFFSETS = ((0, 0), (7, 0), (1, 0), (6, 0), (2, 0), (5, 0), (3, 0), (4, 0), (4, 64))


def product(own, other, slabs):
    n = 16 + len(slabs)
    return pl.pallas_call(
        product_kernel,
        in_specs=[pl.BlockSpec(memory_space=pl.ANY)] * (2 + len(slabs)),
        out_specs=pl.BlockSpec(memory_space=pltpu.VMEM),
        out_shape=jax.ShapeDtypeStruct((8, 128, 1024), jnp.int16),
        scratch_shapes=[
            pltpu.VMEM((1024, 2048), jnp.bfloat16),
            pltpu.VMEM((2048, 1024), jnp.bfloat16),
            pltpu.SemaphoreType.DMA((n,)),
        ],
        compiler_params=pltpu.CompilerParams(vmem_limit_bytes=40 * 2**20),
        cost_estimate=pl.CostEstimate(flops=2 * 1024 * 2048 * 1024, bytes_accessed=10 * 2**20, transcendentals=2**20),
        name="product",
    )(own, other, *slabs)


def square_kernel(bad, q_ref, s_ref, sum_ref):
    total = decode(q_ref[0])
    for i in range(1, 8):
        total = total + decode(q_ref[i])
    s = total * total
    s_ref[...] = s
    sum_ref[...] = jnp.sum(s, axis=0, keepdims=True) + bad[0]


def squares(q, bad):
    return pl.pallas_call(
        square_kernel,
        grid=(4,),
        in_specs=[
            pl.BlockSpec(memory_space=pltpu.SMEM),
            pl.BlockSpec((8, 128, 256), lambda i: (0, 0, i)),
        ],
        out_specs=[pl.BlockSpec((128, 256), lambda i: (0, i)), pl.BlockSpec((1, 256), lambda i: (0, i))],
        out_shape=[jax.ShapeDtypeStruct((128, 1024), jnp.float32), jax.ShapeDtypeStruct((1, 1024), jnp.float32)],
        name="squares",
    )(bad, q)


def gather_slab(block):
    up = functools.partial(lax.ppermute, axis_name="z", perm=[(i, (i + 1) % NZ) for i in range(NZ)])
    down = functools.partial(lax.ppermute, axis_name="z", perm=[(i, (i - 1) % NZ) for i in range(NZ)])
    p1, n1 = up(block), down(block)
    p2, n2 = up(p1), down(n1)
    p3, n3 = up(p2), down(n2)
    p4, n4 = up(p3[:64]), down(n3[64:])
    mine = [block, p1, n1, p2, n2, p3, n3, p4, n4]
    return mine + [lax.ppermute(b, "xh", [(0, 1), (1, 0)]) for b in mine]


def finish(own, other, right, bad):
    codes = product(own, other, right)
    codes = lax.all_to_all(codes, ("y", "xl"), 0, 0, tiled=True)
    squared, sums = squares(codes, bad)
    for axes, n in ((("y", "xl", "xh"), 16), ("z", 8)):
        sums = lax.all_to_all(jnp.broadcast_to(sums[None], (n, 1, 1024)), axes, 0, 0, tiled=True)
        sums = jnp.sum(sums, axis=0)
    return squared, sums


def inflate(squared, sums):
    return squared / (sums / 16384.0 + 1e-06)


def swap_core(x):
    return lax.ppermute(x, "core", [(0, 1), (1, 0)])


def dense(markov, markov_tiles, slab, slab_tiles):
    right = gather_slab(masked(slab, slab_tiles, 128))
    left = masked(markov, markov_tiles, 1024).reshape(NZ, 1024, 128)
    own = lax.all_to_all(left, "z", 0, 0, tiled=True)
    return inflate(*finish(own, swap_core(own), right, jnp.zeros((1,), jnp.float32)))


def per_device(markov, markov_tiles, slab, slab_tiles):
    right = gather_slab(masked(slab, slab_tiles, 128))
    own = lax.all_to_all(pack(markov, markov_tiles), "z", 0, 0, tiled=True)
    other = swap_core(own)
    own_flags, other_flags = flags_of(own), flags_of(other)
    counts = jnp.maximum(jnp.max(jnp.sum(own_flags, axis=1)), jnp.max(jnp.sum(other_flags, axis=1)))
    bad = jnp.where(counts > CAP, jnp.inf, 0.0).astype(jnp.float32).reshape(1)
    squared, sums = finish(
        unpack(own, own_flags.reshape(-1)), unpack(other, other_flags.reshape(-1)), right, bad
    )
    return lax.cond(
        sums[0, 0] > 1e30,
        lambda: dense(markov, markov_tiles, slab, slab_tiles),
        lambda: inflate(squared, sums),
    )


def solution(mesh):
    fine = Mesh(mesh.devices.reshape(NZ, NY, NX, 2, 2), ("z", "y", "xl", "xh", "core"))
    layer = ("z", "y", "xl")
    in_specs = (
        P("xh", layer + ("core",)),
        P("xh", layer + ("core",)),
        P(layer + ("xh",), "core"),
        P(layer + ("xh",), "core"),
    )
    return jax.shard_map(
        per_device, mesh=fine, in_specs=in_specs, out_specs=P(("xh",) + layer, "core"), check_vma=False
    )
```

```python
import functools

import jax
import jax.numpy as jnp
from jax import lax
from jax.experimental import pallas as pl
from jax.experimental.pallas import tpu as pltpu
from jax.sharding import Mesh
from jax.sharding import PartitionSpec as P

NZ, NY, NX = 8, 4, 2
TILE = 64
CAP = 21
SLAB_CAP = 20
PARTS = 1
ALL = ("z", "y", "xl", "xh")
LOW = -2.75
STEP = 13.8 / 65534.0


def lanes(rows):
    return lax.broadcasted_iota(jnp.int32, (rows, 128), 1) < TILE


def mask_kernel(tiles, x_ref, o_ref):
    rows, cols = x_ref.shape
    half = lanes(TILE)
    base = pl.program_id(0) * (rows // TILE)
    for i in range(rows // TILE):
        for g in range(cols // 128):
            keep = jnp.where(half, tiles[base + i, 2 * g], tiles[base + i, 2 * g + 1])
            at = (pl.ds(i * TILE, TILE), pl.ds(g * 128, 128))
            x = x_ref[at].astype(jnp.float32)
            o_ref[at] = jnp.where(keep != 0, x, 0.0).astype(o_ref.dtype)


def masked(x, tiles, block):
    return pl.pallas_call(
        mask_kernel,
        grid=(x.shape[0] // block,),
        in_specs=[
            pl.BlockSpec(memory_space=pltpu.SMEM),
            pl.BlockSpec((block, x.shape[1]), lambda i: (i, 0)),
        ],
        out_specs=pl.BlockSpec((block, x.shape[1]), lambda i: (i, 0)),
        out_shape=jax.ShapeDtypeStruct(x.shape, x.dtype),
        name="mask",
    )(tiles, x)


def halves(x):
    return jnp.concatenate([x[:, TILE:], x[:, :TILE]], axis=1)


def half_masks(dtype):
    left = (lax.broadcasted_iota(jnp.int32, (16, 128), 1) < TILE).astype(jnp.float32)
    return left.astype(dtype), (1.0 - left).astype(dtype)


def keep(f0, f1, dtype):
    return jnp.where(lanes(TILE), f0, f1).astype(jnp.float32).astype(dtype)


def slot_parts(base, slot):
    rows = pl.ds(pl.multiple_of(base + 16 * (slot // 4), 16), 16)
    col = 256 * (slot % 4)
    return tuple((rows, pl.ds(pl.multiple_of(col + 128 * k, 128), 128)) for k in range(2))


def put_pair(ref, base, slot, cap, f0, f1, read):
    left, right = half_masks(ref.dtype)

    @pl.when((f0 > 0) & (slot < cap))
    def _():
        for k, at in enumerate(slot_parts(base, slot)):
            ref[at] = read(2 * k) * left + halves(read(2 * k + 1)) * right

    @pl.when((f1 > 0) & (slot + f0 < cap))
    def _():
        for k, at in enumerate(slot_parts(base, slot + f0)):
            ref[at] = halves(read(2 * k)) * left + read(2 * k + 1) * right


def take_pairs(ref, base, cap, slot, flags, outs):
    left, right = half_masks(ref.dtype)
    loaded = []
    for f0, f1 in flags:
        pair = []
        for f in (f0, f1):
            pair.append([ref[at] for at in slot_parts(base, jnp.minimum(slot, cap - 1))])
            slot = slot + f
        loaded.append(pair)
    for (f0, f1), (a, b), out in zip(flags, loaded, outs):
        zero = jnp.zeros((16, 128), jnp.float32)
        l = left * (zero + f0.astype(jnp.float32)).astype(ref.dtype)
        r = right * (zero + f1.astype(jnp.float32)).astype(ref.dtype)
        for k in range(2):
            out(2 * k, a[k] * l + halves(b[k]) * r)
            out(2 * k + 1, halves(a[k]) * l + b[k] * r)
    return slot


def pack_slab_kernel(tiles, x_ref, o_ref):
    o_ref[...] = jnp.zeros_like(o_ref)
    slot = 0
    row = lax.broadcasted_iota(jnp.int32, (16, 128), 0)
    lane = lax.broadcasted_iota(jnp.int32, (16, 128), 1)
    flags = jnp.zeros((16, 128), jnp.int32)
    for i in range(2):
        for g in range(8):
            f0, f1 = tiles[i, 2 * g], tiles[i, 2 * g + 1]

            def read(q, i=i, g=g):
                return x_ref[pl.ds(i * TILE + 16 * q, 16), pl.ds(g * 128, 128)]

            put_pair(o_ref, 0, slot, SLAB_CAP, f0, f1, read)
            slot = slot + f0 + f1
            for j, f in enumerate((f0, f1)):
                here = (row == i) & (lane == 16 + 2 * g + j)
                flags = jnp.where(here, f, flags)
    o_ref[pl.ds(80, 16), pl.ds(512, 128)] = flags.astype(jnp.float32).astype(o_ref.dtype)


def pack_slab(slab, tiles):
    return pl.pallas_call(
        pack_slab_kernel,
        in_specs=[pl.BlockSpec(memory_space=pltpu.SMEM), pl.BlockSpec(memory_space=pltpu.VMEM)],
        out_specs=pl.BlockSpec(memory_space=pltpu.VMEM),
        out_shape=jax.ShapeDtypeStruct((96, 1024), slab.dtype),
        name="pack_slab",
    )(tiles, slab)


def pack_markov_kernel(tiles, slab_tiles, flags_ref, x_ref, slab_ref, up_ref, down_ref, poison_ref):
    dtype = x_ref.dtype
    z = lax.axis_index("z")
    slab_count = 0
    for i in range(2):
        for j in range(16):
            slab_count = slab_count + slab_tiles[i, j]
    fits = slab_count <= SLAB_CAP
    slab_flags = slab_ref[pl.ds(80, 16), :]
    for ref, sign, reach in ((up_ref, 1, 4), (down_ref, -1, 3)):
        ref[pl.ds(96, 80), :] = slab_ref[pl.ds(0, 80), :]
        ref[pl.ds(176, 80), :] = jnp.zeros((80, 1024), dtype)
        ref[pl.ds(256, 16), :] = slab_flags

        def one(t, slot, ref=ref, sign=sign):
            tile = lax.rem(z + sign * (t // 16 + 1) + NZ, NZ) * 16 + lax.rem(t, 16)
            f0, f1 = tiles[tile, 0], tiles[tile, 1]

            @pl.when(f0 + f1 > 0)
            def _():
                def read(q):
                    return x_ref[pl.ds(pl.multiple_of(tile * TILE + 16 * q, 16), 16), :]

                put_pair(ref, 176, slot, CAP, f0, f1, read)

            return slot + f0 + f1

        fits = fits & (lax.fori_loop(0, 16 * reach, one, 0) <= CAP)
        for e in range(reach):
            to = lax.rem(z + sign * (e + 1) + NZ, NZ) * 16
            flags = flags_ref[pl.ds(pl.multiple_of(to, 16), 16), :].astype(jnp.float32).astype(dtype)
            ref[pl.ds(256, 16), pl.ds(512 + 128 * e, 2)] = flags
    poison_ref[...] = jnp.full((16, 128), jnp.where(fits, 0.0, jnp.nan), dtype)


def pack_markov(markov, markov_tiles, slab_tiles, slab):
    payload = jax.ShapeDtypeStruct((272, 1024), markov.dtype)
    return pl.pallas_call(
        pack_markov_kernel,
        in_specs=[pl.BlockSpec(memory_space=pltpu.SMEM)] * 2 + [pl.BlockSpec(memory_space=pltpu.VMEM)] * 3,
        out_specs=[pl.BlockSpec(memory_space=pltpu.VMEM)] * 3,
        out_shape=[payload, payload, jax.ShapeDtypeStruct((16, 128), markov.dtype)],
        compiler_params=pltpu.CompilerParams(vmem_limit_bytes=16 * 2**20),
        cost_estimate=pl.CostEstimate(flops=2**23, bytes_accessed=20 * 2**20, transcendentals=0),
        name="pack_markov",
    )(markov_tiles, slab_tiles, markov_tiles, markov, slab)


def own_rows_kernel(tiles, poison_ref, x_ref, o_ref, block, sem):
    dtype = x_ref.dtype
    z = lax.axis_index("z")
    copy = pltpu.make_async_copy(x_ref.at[pl.ds(pl.multiple_of(z * 1024, 1024), 1024), :], block, sem)
    copy.start()
    copy.wait()
    poison = poison_ref[pl.ds(0, 1), :]
    for i in range(16):
        rows = pl.ds(i * TILE, TILE)
        o_ref[0, rows, :] = block[rows, :] * keep(tiles[z * 16 + i, 0], tiles[z * 16 + i, 1], dtype) + poison


def own_rows(markov, markov_tiles, poison):
    return pl.pallas_call(
        own_rows_kernel,
        in_specs=[
            pl.BlockSpec(memory_space=pltpu.SMEM),
            pl.BlockSpec(memory_space=pltpu.VMEM),
            pl.BlockSpec(memory_space=pl.ANY),
        ],
        out_specs=pl.BlockSpec(memory_space=pltpu.VMEM),
        out_shape=jax.ShapeDtypeStruct((1, 1024, 128), markov.dtype),
        scratch_shapes=[pltpu.VMEM((1024, 128), markov.dtype), pltpu.SemaphoreType.DMA],
        cost_estimate=pl.CostEstimate(flops=2**20, bytes_accessed=4 * 2**20, transcendentals=0),
        name="own_rows",
    )(markov_tiles, poison, markov)


def stage_kernel(step, ref, other_ref, later, slabs_ref, token_ref, *rest):
    words, scalars, sem = rest[-3:]
    start = ref.shape[0] - 176
    groups = [ref[pl.ds(start + 160, 16), pl.ds(512 + 128 * e, 128)].astype(jnp.float32) for e in range(max(step, 1))]
    words[pl.ds(0, 16), :] = groups[-1].astype(jnp.int32)
    words[pl.ds(16, 8), :] = groups[0][:8].astype(jnp.int32)
    words[pl.ds(24, 8), :] = other_ref[pl.ds(80, 16), pl.ds(512, 128)].astype(jnp.float32)[:8].astype(jnp.int32)
    before = jnp.zeros((1, 128), jnp.float32)
    for flags in groups[:-1]:
        before = before + jnp.sum(flags, axis=0, keepdims=True)
    words[pl.ds(32, 8), :] = jnp.broadcast_to(before, (8, 128)).astype(jnp.int32)
    copy = pltpu.make_async_copy(words, scalars, sem)
    copy.start()
    token_ref[...] = jnp.zeros(token_ref.shape, token_ref.dtype)
    copy.wait()
    for h, (source, base) in enumerate(((ref, start), (other_ref, 0))):
        slot = 0
        for i in range(2):
            for g0 in range(0, 8, 4):
                flags, outs = [], []
                for g in range(g0, g0 + 4):
                    flags.append((scalars[16 + 8 * h + i, 16 + 2 * g], scalars[16 + 8 * h + i, 17 + 2 * g]))

                    def out(q, x, h=h, i=i, g=g):
                        slabs_ref[0, h, pl.ds(i * TILE + 16 * q, 16), pl.ds(128 * g, 128)] = x

                    outs.append(out)
                slot = take_pairs(source, base, SLAB_CAP, slot, flags, outs)
    if step > 0:
        slot = scalars[32, 0] + scalars[32, 1]
        for i0 in range(0, 16, 4):
            flags, outs = [], []
            for i in range(i0, i0 + 4):
                flags.append((scalars[i, 0], scalars[i, 1]))

                def out(q, x, i=i):
                    rest[0][0, pl.ds(i * TILE + 16 * q, 16), :] = x

                outs.append(out)
            slot = take_pairs(ref, start + 80, CAP, slot, flags, outs)


def stage(step, source, other, later):
    dtype = source.dtype
    shapes = [
        jax.ShapeDtypeStruct((1, 2, 128, 1024), dtype),
        jax.ShapeDtypeStruct((16, 128), dtype),
        jax.ShapeDtypeStruct((1, 1024, 128), dtype),
    ]
    shapes = shapes if step > 0 else shapes[:2]
    return pl.pallas_call(
        functools.partial(stage_kernel, step),
        in_specs=[pl.BlockSpec(memory_space=pltpu.VMEM)] * 3,
        out_specs=[pl.BlockSpec(memory_space=pltpu.VMEM)] * len(shapes),
        out_shape=shapes,
        scratch_shapes=[
            pltpu.VMEM((40, 128), jnp.int32),
            pltpu.SMEM((40, 128), jnp.int32),
            pltpu.SemaphoreType.DMA,
        ],
        compiler_params=pltpu.CompilerParams(vmem_limit_bytes=16 * 2**20),
        cost_estimate=pl.CostEstimate(flops=2**23, bytes_accessed=100 * 2**20, transcendentals=0),
        name="stage",
    )(source, other, later)


def encode(p):
    code = jnp.round((jnp.log2(jnp.maximum(p, 0.15)) - LOW) * (1.0 / STEP)) - 32767.0
    code = jnp.where(p > 0.0, code, jnp.where(p == 0.0, -32768.0, 32767.0))
    return code.astype(jnp.int32).astype(jnp.int16)


def decode(q):
    f = q.astype(jnp.int32).astype(jnp.float32)
    p = jnp.exp2((f + 32767.0) * STEP + LOW)
    return jnp.where(f > -32768.0, jnp.where(f < 32767.0, p, jnp.inf), 0.0)


def product_kernel(n, part, *refs):
    lefts, slabs = (refs[:n], refs[n : 2 * n]), refs[2 * n : 3 * n]
    out_ref, left, right, sems = refs[3 * n :]
    cols = pl.ds(part * right.shape[1], right.shape[1])
    z = lax.axis_index("z")
    same = lax.axis_index("xh") == lax.axis_index("core")
    copies = []

    def copy(src, dst):
        copies.append(pltpu.make_async_copy(src, dst, sems.at[len(copies)]))
        copies[-1].start()

    for other in range(2):
        slot = jnp.where(same, other, 1 - other)
        for i, block in enumerate(BLOCKS[n]):
            for k, d in enumerate(block):
                place = lax.rem(z + d, NZ) * 256
                copy(lefts[other][i].at[k], left.at[:, pl.ds(pl.multiple_of(place + 128 * other, 128), 128)])
                rows = pl.ds(pl.multiple_of(place + 128 * slot, 128), 128)
                copy(slabs[i].at[k, other, :, cols], right.at[rows, :])
    for c in copies:
        c.wait()
    rows = 256
    for m in range(1024 // rows):
        p = jnp.dot(left[pl.ds(m * rows, rows), :], right[...], preferred_element_type=jnp.float32)
        q = encode(p)
        for i in range(rows // 128):
            out_ref[m * rows // 128 + i] = q[i * 128 : (i + 1) * 128]


BLOCKS = {8: ((0,), (7,), (1,), (6,), (2,), (5,), (3,), (4,)), 1: ((0, 1, 2, 3, 4, 5, 6, 7),)}


def product(part, left, other_left, right):
    n = len(left)
    width = 1024 // PARTS
    return pl.pallas_call(
        functools.partial(product_kernel, n, part),
        in_specs=[pl.BlockSpec(memory_space=pl.ANY)] * (3 * n),
        out_specs=pl.BlockSpec(memory_space=pltpu.VMEM),
        out_shape=jax.ShapeDtypeStruct((8, 128, width), jnp.int16),
        scratch_shapes=[
            pltpu.VMEM((1024, 2048), jnp.bfloat16),
            pltpu.VMEM((2048, width), jnp.bfloat16),
            pltpu.SemaphoreType.DMA((32,)),
        ],
        compiler_params=pltpu.CompilerParams(vmem_limit_bytes=20 * 2**20),
        cost_estimate=pl.CostEstimate(
            flops=2 * 1024 * 2048 * width, bytes_accessed=10 * 2**20, transcendentals=1024 * width
        ),
        name="product",
    )(*left, *other_left, *right)


def square_kernel(q_ref, s_ref, sum_ref):
    for c in range(0, s_ref.shape[1], 256):
        cols = pl.ds(c, 256)
        sums = jnp.zeros((16, 256), jnp.float32)
        for r in range(0, 128, 16):
            rows = pl.ds(r, 16)
            total = decode(q_ref[0, rows, cols])
            for i in range(1, 8):
                total = total + decode(q_ref[i, rows, cols])
            s = total * total
            s_ref[rows, cols] = s
            sums = sums + s
        sums = jnp.sum(sums, axis=0, keepdims=True)[None]
        sum_ref[:, :, cols] = jnp.broadcast_to(sums, (128, 1, 256))


def squares(q):
    width = q.shape[2]
    return pl.pallas_call(
        square_kernel,
        in_specs=[pl.BlockSpec(memory_space=pltpu.VMEM)],
        out_specs=[pl.BlockSpec(memory_space=pltpu.VMEM)] * 2,
        out_shape=[jax.ShapeDtypeStruct((128, width), jnp.float32), jax.ShapeDtypeStruct((128, 1, width), jnp.float32)],
        cost_estimate=pl.CostEstimate(flops=2**24, bytes_accessed=10 * 2**20, transcendentals=1024 * width),
        name="squares",
    )(q)


def up(x):
    return lax.ppermute(x, "z", [(i, (i + 1) % NZ) for i in range(NZ)])


def down(x):
    return lax.ppermute(x, "z", [(i, (i - 1) % NZ) for i in range(NZ)])


def across(x):
    return lax.ppermute(x, "xh", [(0, 1), (1, 0)])


def swap_core(x):
    return lax.ppermute(x, "core", [(0, 1), (1, 0)])


def exchange(left, right):
    other = [swap_core(x) for x in left]
    parts = []
    for part in range(PARTS):
        codes = product(part, left, other, right)
        parts.append(squares(lax.all_to_all(codes, ("y", "xl"), 0, 0, tiled=True)))
    sums = jnp.concatenate([b for _, b in parts], axis=2)
    return [a for a, _ in parts], jnp.sum(lax.all_to_all(sums, ALL, 0, 0, tiled=True), axis=0)


def inflate(squared, sums):
    return jnp.concatenate(squared, axis=1) / (sums / 16384.0 + 1e-06)


def dense(markov, markov_tiles, slab, slab_tiles):
    left = masked(markov, markov_tiles, 1024).reshape(NZ, 1024, 128)
    left = lax.all_to_all(left, "z", 0, 0, tiled=True)
    left = jnp.roll(left, -lax.axis_index("z"), axis=0)
    own = masked(slab, slab_tiles, 128)
    blocks = [jnp.stack([own, across(own)])]
    for _ in range(NZ - 1):
        blocks.append(down(blocks[-1]))
    return inflate(*exchange([left], [jnp.stack(blocks)]))


def per_device(markov, markov_tiles, slab, slab_tiles):
    own = pack_slab(slab, slab_tiles)
    other = across(own)
    p, n, poison = pack_markov(markov, markov_tiles, slab_tiles, own)
    p, n = (lax.dynamic_update_slice(x, other, (0, 0)) for x in (p, n))
    right, token = stage(0, p, p, poison)
    lefts, rights = [own_rows(markov, markov_tiles, poison)], [right]
    for step in range(1, 5):
        if step < 4:
            p, n = up(p), down(n)
            p, n = (lax.dynamic_update_slice(x, token, (256, 256)) for x in (p, n))
            arrived = [(p, p), (n, n)]
        else:
            arrived = [(up(p[96:]), down(n[:96]))]
        for x, other in arrived:
            right, token, left = stage(step, x, other, token)
            lefts.append(left)
            rights.append(right)
    squared, sums = exchange(lefts, rights)
    return lax.cond(
        sums[0, 0] < 1e30,
        lambda: inflate(squared, sums),
        lambda: dense(markov, markov_tiles, slab, slab_tiles),
    )


def solution(mesh):
    fine = Mesh(mesh.devices.reshape(NZ, NY, NX, 2, 2), ("z", "y", "xl", "xh", "core"))
    layer = ("z", "y", "xl")
    in_specs = (
        P("xh", layer + ("core",)),
        P("xh", layer + ("core",)),
        P(layer + ("xh",), "core"),
        P(layer + ("xh",), "core"),
    )
    return jax.shard_map(
        per_device, mesh=fine, in_specs=in_specs, out_specs=P(("xh",) + layer, "core"), check_vma=False
    )
```

```python
import functools

import jax
import jax.numpy as jnp
from jax import lax
from jax.experimental import pallas as pl
from jax.experimental.pallas import tpu as pltpu
from jax.sharding import Mesh
from jax.sharding import PartitionSpec as P

NZ, NY, NX = 8, 4, 2
TILE = 64
CAP = 21
SLAB_CAP = 20
PARTS = 1
ALL = ("z", "y", "xl", "xh")
LOW = -2.75
STEP = 13.8 / 65534.0


def lanes(rows):
    return lax.broadcasted_iota(jnp.int32, (rows, 128), 1) < TILE


def mask_kernel(tiles, x_ref, o_ref):
    rows, cols = x_ref.shape
    half = lanes(TILE)
    base = pl.program_id(0) * (rows // TILE)
    for i in range(rows // TILE):
        for g in range(cols // 128):
            keep = jnp.where(half, tiles[base + i, 2 * g], tiles[base + i, 2 * g + 1])
            at = (pl.ds(i * TILE, TILE), pl.ds(g * 128, 128))
            x = x_ref[at].astype(jnp.float32)
            o_ref[at] = jnp.where(keep != 0, x, 0.0).astype(o_ref.dtype)


def masked(x, tiles, block):
    return pl.pallas_call(
        mask_kernel,
        grid=(x.shape[0] // block,),
        in_specs=[
            pl.BlockSpec(memory_space=pltpu.SMEM),
            pl.BlockSpec((block, x.shape[1]), lambda i: (i, 0)),
        ],
        out_specs=pl.BlockSpec((block, x.shape[1]), lambda i: (i, 0)),
        out_shape=jax.ShapeDtypeStruct(x.shape, x.dtype),
        name="mask",
    )(tiles, x)


def halves(x):
    return jnp.concatenate([x[:, TILE:], x[:, :TILE]], axis=1)


def half_masks(dtype):
    left = (lax.broadcasted_iota(jnp.int32, (16, 128), 1) < TILE).astype(jnp.float32)
    return left.astype(dtype), (1.0 - left).astype(dtype)


def keep(f0, f1, dtype):
    return jnp.where(lanes(TILE), f0, f1).astype(jnp.float32).astype(dtype)


def slot_parts(base, slot):
    rows = pl.ds(pl.multiple_of(base + 16 * (slot // 4), 16), 16)
    col = 256 * (slot % 4)
    return tuple((rows, pl.ds(pl.multiple_of(col + 128 * k, 128), 128)) for k in range(2))


def put_pair(ref, base, slot, cap, f0, f1, read):
    left, right = half_masks(ref.dtype)

    @pl.when((f0 > 0) & (slot < cap))
    def _():
        for k, at in enumerate(slot_parts(base, slot)):
            ref[at] = read(2 * k) * left + halves(read(2 * k + 1)) * right

    @pl.when((f1 > 0) & (slot + f0 < cap))
    def _():
        for k, at in enumerate(slot_parts(base, slot + f0)):
            ref[at] = halves(read(2 * k)) * left + read(2 * k + 1) * right


def take_pairs(ref, base, cap, slot, flags, outs):
    left, right = half_masks(ref.dtype)
    loaded = []
    for f0, f1 in flags:
        pair = []
        for f in (f0, f1):
            pair.append([ref[at] for at in slot_parts(base, jnp.minimum(slot, cap - 1))])
            slot = slot + f
        loaded.append(pair)
    for (f0, f1), (a, b), out in zip(flags, loaded, outs):
        zero = jnp.zeros((16, 128), jnp.float32)
        l = left * (zero + f0.astype(jnp.float32)).astype(ref.dtype)
        r = right * (zero + f1.astype(jnp.float32)).astype(ref.dtype)
        for k in range(2):
            out(2 * k, a[k] * l + halves(b[k]) * r)
            out(2 * k + 1, halves(a[k]) * l + b[k] * r)
    return slot


def pack_slab_kernel(tiles, x_ref, o_ref):
    o_ref[...] = jnp.zeros_like(o_ref)
    slot = 0
    row = lax.broadcasted_iota(jnp.int32, (16, 128), 0)
    lane = lax.broadcasted_iota(jnp.int32, (16, 128), 1)
    flags = jnp.zeros((16, 128), jnp.int32)
    for i in range(2):
        for g in range(8):
            f0, f1 = tiles[i, 2 * g], tiles[i, 2 * g + 1]

            def read(q, i=i, g=g):
                return x_ref[pl.ds(i * TILE + 16 * q, 16), pl.ds(g * 128, 128)]

            put_pair(o_ref, 0, slot, SLAB_CAP, f0, f1, read)
            slot = slot + f0 + f1
            for j, f in enumerate((f0, f1)):
                here = (row == i) & (lane == 16 + 2 * g + j)
                flags = jnp.where(here, f, flags)
    o_ref[pl.ds(80, 16), pl.ds(512, 128)] = flags.astype(jnp.float32).astype(o_ref.dtype)


def pack_slab(slab, tiles):
    return pl.pallas_call(
        pack_slab_kernel,
        in_specs=[pl.BlockSpec(memory_space=pltpu.SMEM), pl.BlockSpec(memory_space=pltpu.VMEM)],
        out_specs=pl.BlockSpec(memory_space=pltpu.VMEM),
        out_shape=jax.ShapeDtypeStruct((96, 1024), slab.dtype),
        name="pack_slab",
    )(tiles, slab)


def pack_markov_kernel(tiles, slab_tiles, flags_ref, x_ref, slab_ref, up_ref, down_ref, poison_ref):
    dtype = x_ref.dtype
    z = lax.axis_index("z")
    slab_count = 0
    for i in range(2):
        for j in range(16):
            slab_count = slab_count + slab_tiles[i, j]
    fits = slab_count <= SLAB_CAP
    slab_flags = slab_ref[pl.ds(80, 16), :]
    for ref, sign, reach in ((up_ref, 1, 4), (down_ref, -1, 3)):
        ref[pl.ds(96, 80), :] = slab_ref[pl.ds(0, 80), :]
        ref[pl.ds(176, 80), :] = jnp.zeros((80, 1024), dtype)
        ref[pl.ds(256, 16), :] = slab_flags

        def one(t, slot, ref=ref, sign=sign):
            tile = lax.rem(z + sign * (t // 16 + 1) + NZ, NZ) * 16 + lax.rem(t, 16)
            f0, f1 = tiles[tile, 0], tiles[tile, 1]

            @pl.when(f0 + f1 > 0)
            def _():
                def read(q):
                    return x_ref[pl.ds(pl.multiple_of(tile * TILE + 16 * q, 16), 16), :]

                put_pair(ref, 176, slot, CAP, f0, f1, read)

            return slot + f0 + f1

        fits = fits & (lax.fori_loop(0, 16 * reach, one, 0) <= CAP)
        for e in range(reach):
            to = lax.rem(z + sign * (e + 1) + NZ, NZ) * 16
            flags = flags_ref[pl.ds(pl.multiple_of(to, 16), 16), :].astype(jnp.float32).astype(dtype)
            ref[pl.ds(256, 16), pl.ds(512 + 128 * e, 2)] = flags
    poison_ref[...] = jnp.full((16, 128), jnp.where(fits, 0.0, jnp.nan), dtype)


def pack_markov(markov, markov_tiles, slab_tiles, slab):
    payload = jax.ShapeDtypeStruct((272, 1024), markov.dtype)
    return pl.pallas_call(
        pack_markov_kernel,
        in_specs=[pl.BlockSpec(memory_space=pltpu.SMEM)] * 2 + [pl.BlockSpec(memory_space=pltpu.VMEM)] * 3,
        out_specs=[pl.BlockSpec(memory_space=pltpu.VMEM)] * 3,
        out_shape=[payload, payload, jax.ShapeDtypeStruct((16, 128), markov.dtype)],
        compiler_params=pltpu.CompilerParams(vmem_limit_bytes=16 * 2**20),
        cost_estimate=pl.CostEstimate(flops=2**23, bytes_accessed=20 * 2**20, transcendentals=0),
        name="pack_markov",
    )(markov_tiles, slab_tiles, markov_tiles, markov, slab)


def own_rows_kernel(tiles, poison_ref, x_ref, o_ref, block, sem):
    dtype = x_ref.dtype
    z = lax.axis_index("z")
    copy = pltpu.make_async_copy(x_ref.at[pl.ds(pl.multiple_of(z * 1024, 1024), 1024), :], block, sem)
    copy.start()
    copy.wait()
    poison = poison_ref[pl.ds(0, 1), :]
    for i in range(16):
        rows = pl.ds(i * TILE, TILE)
        o_ref[0, rows, :] = block[rows, :] * keep(tiles[z * 16 + i, 0], tiles[z * 16 + i, 1], dtype) + poison


def own_rows(markov, markov_tiles, poison):
    return pl.pallas_call(
        own_rows_kernel,
        in_specs=[
            pl.BlockSpec(memory_space=pltpu.SMEM),
            pl.BlockSpec(memory_space=pltpu.VMEM),
            pl.BlockSpec(memory_space=pl.ANY),
        ],
        out_specs=pl.BlockSpec(memory_space=pltpu.VMEM),
        out_shape=jax.ShapeDtypeStruct((1, 1024, 128), markov.dtype),
        scratch_shapes=[pltpu.VMEM((1024, 128), markov.dtype), pltpu.SemaphoreType.DMA],
        cost_estimate=pl.CostEstimate(flops=2**20, bytes_accessed=4 * 2**20, transcendentals=0),
        name="own_rows",
    )(markov_tiles, poison, markov)


def stage_kernel(step, ref, other_ref, later, slabs_ref, token_ref, *rest):
    words, scalars, sem = rest[-3:]
    start = ref.shape[0] - 176
    groups = [ref[pl.ds(start + 160, 16), pl.ds(512 + 128 * e, 128)].astype(jnp.float32) for e in range(max(step, 1))]
    words[pl.ds(0, 16), :] = groups[-1].astype(jnp.int32)
    words[pl.ds(16, 8), :] = groups[0][:8].astype(jnp.int32)
    words[pl.ds(24, 8), :] = other_ref[pl.ds(80, 16), pl.ds(512, 128)].astype(jnp.float32)[:8].astype(jnp.int32)
    before = jnp.zeros((1, 128), jnp.float32)
    for flags in groups[:-1]:
        before = before + jnp.sum(flags, axis=0, keepdims=True)
    words[pl.ds(32, 8), :] = jnp.broadcast_to(before, (8, 128)).astype(jnp.int32)
    copy = pltpu.make_async_copy(words, scalars, sem)
    copy.start()
    token_ref[...] = jnp.zeros(token_ref.shape, token_ref.dtype)
    copy.wait()
    for h, (source, base) in enumerate(((ref, start), (other_ref, 0))):
        slot = 0
        for i in range(2):
            for g0 in range(0, 8, 4):
                flags, outs = [], []
                for g in range(g0, g0 + 4):
                    flags.append((scalars[16 + 8 * h + i, 16 + 2 * g], scalars[16 + 8 * h + i, 17 + 2 * g]))

                    def out(q, x, h=h, i=i, g=g):
                        slabs_ref[0, h, pl.ds(i * TILE + 16 * q, 16), pl.ds(128 * g, 128)] = x

                    outs.append(out)
                slot = take_pairs(source, base, SLAB_CAP, slot, flags, outs)
    if step > 0:
        slot = scalars[32, 0] + scalars[32, 1]
        for i0 in range(0, 16, 4):
            flags, outs = [], []
            for i in range(i0, i0 + 4):
                flags.append((scalars[i, 0], scalars[i, 1]))

                def out(q, x, i=i):
                    rest[0][0, pl.ds(i * TILE + 16 * q, 16), :] = x

                outs.append(out)
            slot = take_pairs(ref, start + 80, CAP, slot, flags, outs)


def stage(step, source, other, later):
    dtype = source.dtype
    shapes = [
        jax.ShapeDtypeStruct((1, 2, 128, 1024), dtype),
        jax.ShapeDtypeStruct((16, 128), dtype),
        jax.ShapeDtypeStruct((1, 1024, 128), dtype),
    ]
    shapes = shapes if step > 0 else shapes[:2]
    return pl.pallas_call(
        functools.partial(stage_kernel, step),
        in_specs=[pl.BlockSpec(memory_space=pltpu.VMEM)] * 2 + [pl.BlockSpec(memory_space=pl.ANY)],
        out_specs=[pl.BlockSpec(memory_space=pltpu.VMEM)] * len(shapes),
        out_shape=shapes,
        scratch_shapes=[
            pltpu.VMEM((40, 128), jnp.int32),
            pltpu.SMEM((40, 128), jnp.int32),
            pltpu.SemaphoreType.DMA,
        ],
        compiler_params=pltpu.CompilerParams(vmem_limit_bytes=16 * 2**20),
        cost_estimate=pl.CostEstimate(flops=2**23, bytes_accessed=100 * 2**20, transcendentals=0),
        name="stage",
    )(source, other, later)


def encode(p):
    code = jnp.round((jnp.log2(jnp.maximum(p, 0.15)) - LOW) * (1.0 / STEP)) - 32767.0
    code = jnp.where(p > 0.0, code, jnp.where(p == 0.0, -32768.0, 32767.0))
    return code.astype(jnp.int32).astype(jnp.int16)


def decode(q):
    f = q.astype(jnp.int32).astype(jnp.float32)
    p = jnp.exp2((f + 32767.0) * STEP + LOW)
    return jnp.where(f > -32768.0, jnp.where(f < 32767.0, p, jnp.inf), 0.0)


def product_kernel(counts, part, first, last, *refs):
    n = len(counts)
    lefts, slabs = (refs[:n], refs[n : 2 * n]), refs[2 * n : 3 * n]
    earlier = None if first else refs[3 * n]
    out_ref, left, right, acc, sems, acc_sems = refs[-6:]
    width = right.shape[1]
    cols = pl.ds(part * width, width)
    same = lax.axis_index("xh") == lax.axis_index("core")
    rows = 256
    copies, accs = [], []

    def copy(src, dst):
        copies.append(pltpu.make_async_copy(src, dst, sems.at[len(copies)]))
        copies[-1].start()

    for other in range(2):
        slot = jnp.where(same, other, 1 - other)
        place = 0
        for i, count in enumerate(counts):
            for k in range(count):
                copy(lefts[other][i].at[k], left.at[:, pl.ds(place + 128 * other, 128)])
                at = pl.ds(pl.multiple_of(place + 128 * slot, 128), 128)
                copy(slabs[i].at[k, other, :, cols], right.at[at, :])
                place += 256
    if not first:
        for m in range(1024 // rows):
            at = pl.ds(m * rows, rows)
            accs.append(pltpu.make_async_copy(earlier.at[at, cols], acc.at[at, :], acc_sems.at[m]))
            accs[-1].start()
    for c in copies:
        c.wait()
    for m in range(1024 // rows):
        at = pl.ds(m * rows, rows)
        p = jnp.dot(left[at, :], right[...], preferred_element_type=jnp.float32)
        if not first:
            accs[m].wait()
            p = p + acc[at, :]
        if last:
            q = encode(p)
            for i in range(rows // 128):
                out_ref[m * rows // 128 + i] = q[i * 128 : (i + 1) * 128]
        else:
            out_ref[at, :] = p


def product(left, other_left, right, earlier=None, part=0, parts=1, last=True):
    counts = tuple(x.shape[0] for x in left)
    n, depth, width = len(counts), 256 * sum(counts), 1024 // parts
    operands = [*left, *other_left, *right] + ([] if earlier is None else [earlier])
    if last:
        out = jax.ShapeDtypeStruct((8, 128, width), jnp.int16)
    else:
        out = jax.ShapeDtypeStruct((1024, width), jnp.float32)
    return pl.pallas_call(
        functools.partial(product_kernel, counts, part, earlier is None, last),
        in_specs=[pl.BlockSpec(memory_space=pl.ANY)] * len(operands),
        out_specs=pl.BlockSpec(memory_space=pltpu.VMEM),
        out_shape=out,
        scratch_shapes=[
            pltpu.VMEM((1024, depth), jnp.bfloat16),
            pltpu.VMEM((depth, width), jnp.bfloat16),
            pltpu.VMEM((8 if earlier is None else 1024, width), jnp.float32),
            pltpu.SemaphoreType.DMA((4 * sum(counts),)),
            pltpu.SemaphoreType.DMA((4,)),
        ],
        compiler_params=pltpu.CompilerParams(vmem_limit_bytes=20 * 2**20),
        cost_estimate=pl.CostEstimate(
            flops=2 * 1024 * depth * width, bytes_accessed=10 * 2**20, transcendentals=1024 * width
        ),
        name="product",
    )(*operands)


def square_kernel(q_ref, s_ref, sum_ref):
    for c in range(0, s_ref.shape[1], 256):
        cols = pl.ds(c, 256)
        sums = jnp.zeros((16, 256), jnp.float32)
        for r in range(0, 128, 16):
            rows = pl.ds(r, 16)
            total = decode(q_ref[0, rows, cols])
            for i in range(1, 8):
                total = total + decode(q_ref[i, rows, cols])
            s = total * total
            s_ref[rows, cols] = s
            sums = sums + s
        sums = jnp.sum(sums, axis=0, keepdims=True)[None]
        sum_ref[:, :, cols] = jnp.broadcast_to(sums, (128, 1, 256))


def squares(q):
    width = q.shape[2]
    return pl.pallas_call(
        square_kernel,
        in_specs=[pl.BlockSpec(memory_space=pltpu.VMEM)],
        out_specs=[pl.BlockSpec(memory_space=pltpu.VMEM)] * 2,
        out_shape=[jax.ShapeDtypeStruct((128, width), jnp.float32), jax.ShapeDtypeStruct((128, 1, width), jnp.float32)],
        cost_estimate=pl.CostEstimate(flops=2**24, bytes_accessed=10 * 2**20, transcendentals=1024 * width),
        name="squares",
    )(q)


def up(x):
    return lax.ppermute(x, "z", [(i, (i + 1) % NZ) for i in range(NZ)])


def down(x):
    return lax.ppermute(x, "z", [(i, (i - 1) % NZ) for i in range(NZ)])


def across(x):
    return lax.ppermute(x, "xh", [(0, 1), (1, 0)])


def swap_core(x):
    return lax.ppermute(x, "core", [(0, 1), (1, 0)])


def exchange(left, other_left, right, earlier=None):
    parts = []
    for part in range(PARTS):
        codes = product(left, other_left, right, earlier, part, PARTS)
        parts.append(squares(lax.all_to_all(codes, ("y", "xl"), 0, 0, tiled=True)))
    sums = jnp.concatenate([b for _, b in parts], axis=2)
    return [a for a, _ in parts], jnp.sum(lax.all_to_all(sums, ALL, 0, 0, tiled=True), axis=0)


def inflate(squared, sums):
    return jnp.concatenate(squared, axis=1) / (sums / 16384.0 + 1e-06)


def dense(markov, markov_tiles, slab, slab_tiles):
    left = masked(markov, markov_tiles, 1024).reshape(NZ, 1024, 128)
    left = lax.all_to_all(left, "z", 0, 0, tiled=True)
    left = jnp.roll(left, -lax.axis_index("z"), axis=0)
    own = masked(slab, slab_tiles, 128)
    blocks = [jnp.stack([own, across(own)])]
    for _ in range(NZ - 1):
        blocks.append(down(blocks[-1]))
    return inflate(*exchange([left], [swap_core(left)], [jnp.stack(blocks)]))


def per_device(markov, markov_tiles, slab, slab_tiles):
    own = pack_slab(slab, slab_tiles)
    other = across(own)
    p, n, poison = pack_markov(markov, markov_tiles, slab_tiles, own)
    p, n = (lax.dynamic_update_slice(x, other, (0, 0)) for x in (p, n))
    lefts = [own_rows(markov, markov_tiles, poison)]
    others = [swap_core(lefts[0])]
    right, token = stage(0, p, p, lefts[0])
    rights = [right]
    for step in range(1, 5):
        if step < 4:
            p, n = up(p), down(n)
            p, n = (lax.dynamic_update_slice(x, token, (256, 256)) for x in (p, n))
            arrived = [(p, p), (n, n)]
        else:
            arrived = [(up(p[96:]), down(n[:96]))]
            token = early = product(lefts[:5], others[:5], rights[:5], last=False)
        for x, other in arrived:
            right, token, left = stage(step, x, other, token)
            lefts.append(left)
            others.append(swap_core(left))
            rights.append(right)
    squared, sums = exchange(lefts[5:], others[5:], rights[5:], early)
    return lax.cond(
        sums[0, 0] < 1e30,
        lambda: inflate(squared, sums),
        lambda: dense(markov, markov_tiles, slab, slab_tiles),
    )


def solution(mesh):
    fine = Mesh(mesh.devices.reshape(NZ, NY, NX, 2, 2), ("z", "y", "xl", "xh", "core"))
    layer = ("z", "y", "xl")
    in_specs = (
        P("xh", layer + ("core",)),
        P("xh", layer + ("core",)),
        P(layer + ("xh",), "core"),
        P(layer + ("xh",), "core"),
    )
    return jax.shard_map(
        per_device, mesh=fine, in_specs=in_specs, out_specs=P(("xh",) + layer, "core"), check_vma=False
    )
```

```python
import functools

import jax
import jax.numpy as jnp
from jax import lax
from jax.experimental import pallas as pl
from jax.experimental.pallas import tpu as pltpu
from jax.sharding import Mesh
from jax.sharding import PartitionSpec as P

NZ, NY, NX = 8, 4, 2
TILE = 64
CAP = 21
SLAB_CAP = 19
PARTS = 1
ALL = ("z", "y", "xl", "xh")
LOW = -2.75
STEP = 13.8 / 65534.0


def lanes(rows):
    return lax.broadcasted_iota(jnp.int32, (rows, 128), 1) < TILE


def mask_kernel(tiles, x_ref, o_ref):
    rows, cols = x_ref.shape
    half = lanes(TILE)
    base = pl.program_id(0) * (rows // TILE)
    for i in range(rows // TILE):
        for g in range(cols // 128):
            keep = jnp.where(half, tiles[base + i, 2 * g], tiles[base + i, 2 * g + 1])
            at = (pl.ds(i * TILE, TILE), pl.ds(g * 128, 128))
            x = x_ref[at].astype(jnp.float32)
            o_ref[at] = jnp.where(keep != 0, x, 0.0).astype(o_ref.dtype)


def masked(x, tiles, block):
    return pl.pallas_call(
        mask_kernel,
        grid=(x.shape[0] // block,),
        in_specs=[
            pl.BlockSpec(memory_space=pltpu.SMEM),
            pl.BlockSpec((block, x.shape[1]), lambda i: (i, 0)),
        ],
        out_specs=pl.BlockSpec((block, x.shape[1]), lambda i: (i, 0)),
        out_shape=jax.ShapeDtypeStruct(x.shape, x.dtype),
        name="mask",
    )(tiles, x)


def halves(x):
    return jnp.concatenate([x[:, TILE:], x[:, :TILE]], axis=1)


def half_masks(dtype):
    left = (lax.broadcasted_iota(jnp.int32, (16, 128), 1) < TILE).astype(jnp.float32)
    return left.astype(dtype), (1.0 - left).astype(dtype)


def keep(f0, f1, dtype):
    return jnp.where(lanes(TILE), f0, f1).astype(jnp.float32).astype(dtype)


def slot_parts(base, slot):
    rows = pl.ds(pl.multiple_of(base + 16 * (slot // 4), 16), 16)
    col = 256 * (slot % 4)
    return tuple((rows, pl.ds(pl.multiple_of(col + 128 * k, 128), 128)) for k in range(2))


def put_pair(ref, base, slot, cap, f0, f1, read):
    left, right = half_masks(ref.dtype)

    @pl.when((f0 > 0) & (slot < cap))
    def _():
        for k, at in enumerate(slot_parts(base, slot)):
            ref[at] = read(2 * k) * left + halves(read(2 * k + 1)) * right

    @pl.when((f1 > 0) & (slot + f0 < cap))
    def _():
        for k, at in enumerate(slot_parts(base, slot + f0)):
            ref[at] = halves(read(2 * k)) * left + read(2 * k + 1) * right


def take_pairs(ref, base, cap, slot, flags, outs):
    left, right = half_masks(ref.dtype)
    loaded = []
    for f0, f1 in flags:
        pair = []
        for f in (f0, f1):
            pair.append([ref[at] for at in slot_parts(base, jnp.minimum(slot, cap - 1))])
            slot = slot + f
        loaded.append(pair)
    for (f0, f1), (a, b), out in zip(flags, loaded, outs):
        zero = jnp.zeros((16, 128), jnp.float32)
        l = left * (zero + f0.astype(jnp.float32)).astype(ref.dtype)
        r = right * (zero + f1.astype(jnp.float32)).astype(ref.dtype)
        for k in range(2):
            out(2 * k, a[k] * l + halves(b[k]) * r)
            out(2 * k + 1, halves(a[k]) * l + b[k] * r)
    return slot


def pack_slab_kernel(tiles, x_ref, o_ref):
    o_ref[...] = jnp.zeros_like(o_ref)
    slot = 0
    row = lax.broadcasted_iota(jnp.int32, (16, 128), 0)
    lane = lax.broadcasted_iota(jnp.int32, (16, 128), 1)
    flags = jnp.zeros((16, 128), jnp.int32)
    for i in range(2):
        for g in range(8):
            f0, f1 = tiles[i, 2 * g], tiles[i, 2 * g + 1]

            def read(q, i=i, g=g):
                return x_ref[pl.ds(i * TILE + 16 * q, 16), pl.ds(g * 128, 128)]

            put_pair(o_ref, 0, slot, SLAB_CAP, f0, f1, read)
            slot = slot + f0 + f1
            for j, f in enumerate((f0, f1)):
                here = (row == i) & (lane == 16 + 2 * g + j)
                flags = jnp.where(here, f, flags)
    o_ref[pl.ds(64, 16), pl.ds(768, 128)] = flags.astype(jnp.float32).astype(o_ref.dtype)


def pack_slab(slab, tiles):
    return pl.pallas_call(
        pack_slab_kernel,
        in_specs=[pl.BlockSpec(memory_space=pltpu.SMEM), pl.BlockSpec(memory_space=pltpu.VMEM)],
        out_specs=pl.BlockSpec(memory_space=pltpu.VMEM),
        out_shape=jax.ShapeDtypeStruct((80, 1024), slab.dtype),
        name="pack_slab",
    )(tiles, slab)


def pack_markov_kernel(tiles, slab_tiles, flags_ref, x_ref, slab_ref, up_ref, down_ref, poison_ref):
    dtype = x_ref.dtype
    z = lax.axis_index("z")
    slab_count = 0
    for i in range(2):
        for j in range(16):
            slab_count = slab_count + slab_tiles[i, j]
    fits = slab_count <= SLAB_CAP
    for ref, sign, reach in ((up_ref, 1, 4), (down_ref, -1, 3)):
        ref[pl.ds(80, 80), :] = slab_ref[...]
        ref[pl.ds(160, 96), :] = jnp.zeros((96, 1024), dtype)

        slot = 0
        for e in range(reach):
            to = lax.rem(z + sign * (e + 1) + NZ, NZ) * 16

            def one(t, slot, ref=ref, to=to):
                f0, f1 = tiles[to + t, 0], tiles[to + t, 1]

                @pl.when(f0 + f1 > 0)
                def _():
                    def read(q):
                        return x_ref[pl.ds(pl.multiple_of((to + t) * TILE + 16 * q, 16), 16), :]

                    put_pair(ref, 160, slot, CAP, f0, f1, read)

                return slot + f0 + f1

            slot = lax.fori_loop(0, 16, one, slot, unroll=4)
        fits = fits & (slot <= CAP)
        for e in range(reach):
            to = lax.rem(z + sign * (e + 1) + NZ, NZ) * 16
            flags = flags_ref[pl.ds(pl.multiple_of(to, 16), 16), :].astype(jnp.float32).astype(dtype)
            ref[pl.ds(240, 16), pl.ds(512 + 128 * e, 2)] = flags
    poison_ref[...] = jnp.full((16, 128), jnp.where(fits, 0.0, jnp.nan), dtype)


def pack_markov(markov, markov_tiles, slab_tiles, slab):
    payload = jax.ShapeDtypeStruct((256, 1024), markov.dtype)
    return pl.pallas_call(
        pack_markov_kernel,
        in_specs=[pl.BlockSpec(memory_space=pltpu.SMEM)] * 2 + [pl.BlockSpec(memory_space=pltpu.VMEM)] * 3,
        out_specs=[pl.BlockSpec(memory_space=pltpu.VMEM)] * 3,
        out_shape=[payload, payload, jax.ShapeDtypeStruct((16, 128), markov.dtype)],
        compiler_params=pltpu.CompilerParams(vmem_limit_bytes=16 * 2**20),
        cost_estimate=pl.CostEstimate(flops=2**23, bytes_accessed=20 * 2**20, transcendentals=0),
        name="pack_markov",
    )(markov_tiles, slab_tiles, markov_tiles, markov, slab)


def own_rows_kernel(tiles, poison_ref, x_ref, o_ref, block, sem):
    dtype = x_ref.dtype
    z = lax.axis_index("z")
    copy = pltpu.make_async_copy(x_ref.at[pl.ds(pl.multiple_of(z * 1024, 1024), 1024), :], block, sem)
    copy.start()
    copy.wait()
    poison = poison_ref[pl.ds(0, 1), :]
    for i in range(16):
        rows = pl.ds(i * TILE, TILE)
        o_ref[0, rows, :] = block[rows, :] * keep(tiles[z * 16 + i, 0], tiles[z * 16 + i, 1], dtype) + poison


def own_rows(markov, markov_tiles, poison):
    return pl.pallas_call(
        own_rows_kernel,
        in_specs=[
            pl.BlockSpec(memory_space=pltpu.SMEM),
            pl.BlockSpec(memory_space=pltpu.VMEM),
            pl.BlockSpec(memory_space=pl.ANY),
        ],
        out_specs=pl.BlockSpec(memory_space=pltpu.VMEM),
        out_shape=jax.ShapeDtypeStruct((1, 1024, 128), markov.dtype),
        scratch_shapes=[pltpu.VMEM((1024, 128), markov.dtype), pltpu.SemaphoreType.DMA],
        cost_estimate=pl.CostEstimate(flops=2**20, bytes_accessed=4 * 2**20, transcendentals=0),
        name="own_rows",
    )(markov_tiles, poison, markov)


def stage_kernel(step, ref, other_ref, later, slabs_ref, token_ref, *rest):
    words, scalars, sem = rest[-3:]
    start = ref.shape[0] - 176
    groups = [ref[pl.ds(start + 160, 16), pl.ds(512 + 128 * e, 128)].astype(jnp.float32) for e in range(max(step, 1))]
    words[pl.ds(0, 16), :] = groups[-1].astype(jnp.int32)
    for k, (slab_ref, base) in enumerate(((ref, start), (other_ref, 0))):
        flags = slab_ref[pl.ds(base + 64, 16), pl.ds(768, 128)].astype(jnp.float32)
        words[pl.ds(16 + 8 * k, 8), :] = flags[:8].astype(jnp.int32)
    before = jnp.zeros((1, 128), jnp.float32)
    for flags in groups[:-1]:
        before = before + jnp.sum(flags, axis=0, keepdims=True)
    words[pl.ds(32, 8), :] = jnp.broadcast_to(before, (8, 128)).astype(jnp.int32)
    copy = pltpu.make_async_copy(words, scalars, sem)
    copy.start()
    token_ref[...] = jnp.zeros(token_ref.shape, token_ref.dtype)
    copy.wait()
    for h, (source, base) in enumerate(((ref, start), (other_ref, 0))):
        slot = 0
        for i in range(2):
            for g0 in range(0, 8, 4):
                flags, outs = [], []
                for g in range(g0, g0 + 4):
                    flags.append((scalars[16 + 8 * h + i, 16 + 2 * g], scalars[16 + 8 * h + i, 17 + 2 * g]))

                    def out(q, x, h=h, i=i, g=g):
                        slabs_ref[0, h, pl.ds(i * TILE + 16 * q, 16), pl.ds(128 * g, 128)] = x

                    outs.append(out)
                slot = take_pairs(source, base, SLAB_CAP, slot, flags, outs)
    if step > 0:
        slot = scalars[32, 0] + scalars[32, 1]
        for i0 in range(0, 16, 4):
            flags, outs = [], []
            for i in range(i0, i0 + 4):
                flags.append((scalars[i, 0], scalars[i, 1]))

                def out(q, x, i=i):
                    rest[0][0, pl.ds(i * TILE + 16 * q, 16), :] = x

                outs.append(out)
            slot = take_pairs(ref, start + 80, CAP, slot, flags, outs)


def stage(step, source, other, later):
    dtype = source.dtype
    shapes = [
        jax.ShapeDtypeStruct((1, 2, 128, 1024), dtype),
        jax.ShapeDtypeStruct((16, 128), dtype),
        jax.ShapeDtypeStruct((1, 1024, 128), dtype),
    ]
    shapes = shapes if step > 0 else shapes[:2]
    return pl.pallas_call(
        functools.partial(stage_kernel, step),
        in_specs=[pl.BlockSpec(memory_space=pltpu.VMEM)] * 2 + [pl.BlockSpec(memory_space=pl.ANY)],
        out_specs=[pl.BlockSpec(memory_space=pltpu.VMEM)] * len(shapes),
        out_shape=shapes,
        scratch_shapes=[
            pltpu.VMEM((40, 128), jnp.int32),
            pltpu.SMEM((40, 128), jnp.int32),
            pltpu.SemaphoreType.DMA,
        ],
        compiler_params=pltpu.CompilerParams(vmem_limit_bytes=16 * 2**20),
        cost_estimate=pl.CostEstimate(flops=2**23, bytes_accessed=100 * 2**20, transcendentals=0),
        name="stage",
    )(source, other, later)


def encode(p):
    code = jnp.round((jnp.log2(jnp.maximum(p, 0.15)) - LOW) * (1.0 / STEP)) - 32767.0
    code = jnp.where(p > 0.0, code, jnp.where(p == 0.0, -32768.0, 32767.0))
    return code.astype(jnp.int32).astype(jnp.int16)


def decode(q):
    f = q.astype(jnp.int32).astype(jnp.float32)
    p = jnp.exp2((f + 32767.0) * STEP + LOW)
    return jnp.where(f > -32768.0, jnp.where(f < 32767.0, p, jnp.inf), 0.0)


def product_kernel(counts, part, first, last, *refs):
    n = len(counts)
    lefts, slabs = (refs[:n], refs[n : 2 * n]), refs[2 * n : 3 * n]
    earlier = None if first else refs[3 * n]
    out_ref, left, right, acc, sems, acc_sems = refs[-6:]
    width = right.shape[1]
    cols = pl.ds(part * width, width)
    same = lax.axis_index("xh") == lax.axis_index("core")
    rows = 256
    copies, accs = [], []

    def copy(src, dst):
        copies.append(pltpu.make_async_copy(src, dst, sems.at[len(copies)]))
        copies[-1].start()

    for other in range(2):
        slot = jnp.where(same, other, 1 - other)
        place = 0
        for i, count in enumerate(counts):
            for k in range(count):
                copy(lefts[other][i].at[k], left.at[:, pl.ds(place + 128 * other, 128)])
                at = pl.ds(pl.multiple_of(place + 128 * slot, 128), 128)
                copy(slabs[i].at[k, other, :, cols], right.at[at, :])
                place += 256
    if not first:
        for m in range(1024 // rows):
            at = pl.ds(m * rows, rows)
            accs.append(pltpu.make_async_copy(earlier.at[at, cols], acc.at[at, :], acc_sems.at[m]))
            accs[-1].start()
    for c in copies:
        c.wait()
    for c in accs:
        c.wait()
    for m in range(1024 // rows):
        at = pl.ds(m * rows, rows)
        p = jnp.dot(left[at, :], right[...], preferred_element_type=jnp.float32)
        if not first:
            p = p + acc[at, :]
        if last:
            q = encode(p)
            for i in range(rows // 128):
                out_ref[m * rows // 128 + i] = q[i * 128 : (i + 1) * 128]
        else:
            out_ref[at, :] = p


def product(left, other_left, right, earlier=None, part=0, parts=1, last=True):
    counts = tuple(x.shape[0] for x in left)
    n, depth, width = len(counts), 256 * sum(counts), 1024 // parts
    operands = [*left, *other_left, *right] + ([] if earlier is None else [earlier])
    if last:
        out = jax.ShapeDtypeStruct((8, 128, width), jnp.int16)
    else:
        out = jax.ShapeDtypeStruct((1024, width), jnp.float32)
    return pl.pallas_call(
        functools.partial(product_kernel, counts, part, earlier is None, last),
        in_specs=[pl.BlockSpec(memory_space=pl.ANY)] * len(operands),
        out_specs=pl.BlockSpec(memory_space=pltpu.VMEM),
        out_shape=out,
        scratch_shapes=[
            pltpu.VMEM((1024, depth), jnp.bfloat16),
            pltpu.VMEM((depth, width), jnp.bfloat16),
            pltpu.VMEM((8 if earlier is None else 1024, width), jnp.float32),
            pltpu.SemaphoreType.DMA((4 * sum(counts),)),
            pltpu.SemaphoreType.DMA((4,)),
        ],
        compiler_params=pltpu.CompilerParams(vmem_limit_bytes=20 * 2**20),
        cost_estimate=pl.CostEstimate(
            flops=2 * 1024 * depth * width, bytes_accessed=10 * 2**20, transcendentals=1024 * width
        ),
        name="product",
    )(*operands)


def square_kernel(q_ref, s_ref, sum_ref):
    for c in range(0, s_ref.shape[1], 256):
        cols = pl.ds(c, 256)
        sums = jnp.zeros((16, 256), jnp.float32)
        for r in range(0, 128, 16):
            rows = pl.ds(r, 16)
            total = decode(q_ref[0, rows, cols])
            for i in range(1, 8):
                total = total + decode(q_ref[i, rows, cols])
            s = total * total
            s_ref[rows, cols] = s
            sums = sums + s
        sums = jnp.sum(sums, axis=0, keepdims=True)[None]
        sum_ref[:, :, cols] = jnp.broadcast_to(sums, (128, 1, 256))


def squares(q):
    width = q.shape[2]
    return pl.pallas_call(
        square_kernel,
        in_specs=[pl.BlockSpec(memory_space=pltpu.VMEM)],
        out_specs=[pl.BlockSpec(memory_space=pltpu.VMEM)] * 2,
        out_shape=[jax.ShapeDtypeStruct((128, width), jnp.float32), jax.ShapeDtypeStruct((128, 1, width), jnp.float32)],
        cost_estimate=pl.CostEstimate(flops=2**24, bytes_accessed=10 * 2**20, transcendentals=1024 * width),
        name="squares",
    )(q)


def up(x):
    return lax.ppermute(x, "z", [(i, (i + 1) % NZ) for i in range(NZ)])


def down(x):
    return lax.ppermute(x, "z", [(i, (i - 1) % NZ) for i in range(NZ)])


def across(x):
    return lax.ppermute(x, "xh", [(0, 1), (1, 0)])


def swap_core(x):
    return lax.ppermute(x, "core", [(0, 1), (1, 0)])


def exchange(left, other_left, right, earlier=None):
    parts = []
    for part in range(PARTS):
        codes = product(left, other_left, right, earlier, part, PARTS)
        parts.append(squares(lax.all_to_all(codes, ("y", "xl"), 0, 0, tiled=True)))
    sums = jnp.concatenate([b for _, b in parts], axis=2)
    return [a for a, _ in parts], jnp.sum(lax.all_to_all(sums, ALL, 0, 0, tiled=True), axis=0)


def inflate(squared, sums):
    return jnp.concatenate(squared, axis=1) / (sums / 16384.0 + 1e-06)


def dense(markov, markov_tiles, slab, slab_tiles):
    left = masked(markov, markov_tiles, 1024).reshape(NZ, 1024, 128)
    left = lax.all_to_all(left, "z", 0, 0, tiled=True)
    left = jnp.roll(left, -lax.axis_index("z"), axis=0)
    own = masked(slab, slab_tiles, 128)
    blocks = [jnp.stack([own, across(own)])]
    for _ in range(NZ - 1):
        blocks.append(down(blocks[-1]))
    return inflate(*exchange([left], [swap_core(left)], [jnp.stack(blocks)]))


def per_device(markov, markov_tiles, slab, slab_tiles):
    own = pack_slab(slab, slab_tiles)
    other = across(own)
    p, n, poison = pack_markov(markov, markov_tiles, slab_tiles, own)
    p, n = (lax.dynamic_update_slice(x, other, (0, 0)) for x in (p, n))
    lefts = [own_rows(markov, markov_tiles, poison)]
    others = [swap_core(lefts[0])]
    right, token = stage(0, p, p, lefts[0])
    rights = [right]
    for step in range(1, 5):
        if step < 4:
            p, n = up(p), down(n)
            p, n = (lax.dynamic_update_slice(x, token, (240, 256)) for x in (p, n))
            arrived = [(p, p), (n, n)]
        else:
            arrived = [(up(p[80:]), down(n[:80]))]
            token = early = product(lefts[:5], others[:5], rights[:5], last=False)
        for x, other in arrived:
            right, token, left = stage(step, x, other, token)
            lefts.append(left)
            others.append(swap_core(left))
            rights.append(right)
    squared, sums = exchange(lefts[5:], others[5:], rights[5:], early)
    return lax.cond(
        sums[0, 0] < 1e30,
        lambda: inflate(squared, sums),
        lambda: dense(markov, markov_tiles, slab, slab_tiles),
    )


def solution(mesh):
    fine = Mesh(mesh.devices.reshape(NZ, NY, NX, 2, 2), ("z", "y", "xl", "xh", "core"))
    layer = ("z", "y", "xl")
    in_specs = (
        P("xh", layer + ("core",)),
        P("xh", layer + ("core",)),
        P(layer + ("xh",), "core"),
        P(layer + ("xh",), "core"),
    )
    return jax.shard_map(
        per_device, mesh=fine, in_specs=in_specs, out_specs=P(("xh",) + layer, "core"), check_vma=False
    )
```

```python
import functools

import jax
import jax.numpy as jnp
from jax import lax
from jax.experimental import pallas as pl
from jax.experimental.pallas import tpu as pltpu
from jax.sharding import Mesh
from jax.sharding import PartitionSpec as P

NZ, NY, NX = 8, 4, 2
TILE = 64
CAP = 21
SLAB_CAP = 19
PARTS = 1
ALL = ("z", "y", "xl", "xh")
LOW = -2.75
STEP = 13.8 / 65534.0


def lanes(rows):
    return lax.broadcasted_iota(jnp.int32, (rows, 128), 1) < TILE


def mask_kernel(tiles, x_ref, o_ref):
    rows, cols = x_ref.shape
    half = lanes(TILE)
    base = pl.program_id(0) * (rows // TILE)
    for i in range(rows // TILE):
        for g in range(cols // 128):
            keep = jnp.where(half, tiles[base + i, 2 * g], tiles[base + i, 2 * g + 1])
            at = (pl.ds(i * TILE, TILE), pl.ds(g * 128, 128))
            x = x_ref[at].astype(jnp.float32)
            o_ref[at] = jnp.where(keep != 0, x, 0.0).astype(o_ref.dtype)


def masked(x, tiles, block):
    return pl.pallas_call(
        mask_kernel,
        grid=(x.shape[0] // block,),
        in_specs=[
            pl.BlockSpec(memory_space=pltpu.SMEM),
            pl.BlockSpec((block, x.shape[1]), lambda i: (i, 0)),
        ],
        out_specs=pl.BlockSpec((block, x.shape[1]), lambda i: (i, 0)),
        out_shape=jax.ShapeDtypeStruct(x.shape, x.dtype),
        name="mask",
    )(tiles, x)


def halves(x):
    return jnp.concatenate([x[:, TILE:], x[:, :TILE]], axis=1)


def half_masks(dtype):
    left = (lax.broadcasted_iota(jnp.int32, (16, 128), 1) < TILE).astype(jnp.float32)
    return left.astype(dtype), (1.0 - left).astype(dtype)


def keep(f0, f1, dtype):
    return jnp.where(lanes(TILE), f0, f1).astype(jnp.float32).astype(dtype)


def slot_parts(base, slot):
    rows = pl.ds(pl.multiple_of(base + 16 * (slot // 4), 16), 16)
    col = 256 * (slot % 4)
    return tuple((rows, pl.ds(pl.multiple_of(col + 128 * k, 128), 128)) for k in range(2))


def put_pair(ref, base, slot, cap, f0, f1, read):
    left, right = half_masks(ref.dtype)

    @pl.when((f0 > 0) & (slot < cap))
    def _():
        for k, at in enumerate(slot_parts(base, slot)):
            ref[at] = read(2 * k) * left + halves(read(2 * k + 1)) * right

    @pl.when((f1 > 0) & (slot + f0 < cap))
    def _():
        for k, at in enumerate(slot_parts(base, slot + f0)):
            ref[at] = halves(read(2 * k)) * left + read(2 * k + 1) * right


def take_pairs(ref, base, cap, slot, flags, outs):
    left, right = half_masks(ref.dtype)
    loaded = []
    for f0, f1 in flags:
        pair = []
        for f in (f0, f1):
            pair.append([ref[at] for at in slot_parts(base, jnp.minimum(slot, cap - 1))])
            slot = slot + f
        loaded.append(pair)
    for (f0, f1), (a, b), out in zip(flags, loaded, outs):
        zero = jnp.zeros((16, 128), jnp.float32)
        l = left * (zero + f0.astype(jnp.float32)).astype(ref.dtype)
        r = right * (zero + f1.astype(jnp.float32)).astype(ref.dtype)
        for k in range(2):
            out(2 * k, a[k] * l + halves(b[k]) * r)
            out(2 * k + 1, halves(a[k]) * l + b[k] * r)
    return slot


def pack_slab_kernel(tiles, x_ref, o_ref):
    o_ref[...] = jnp.zeros_like(o_ref)
    slot = 0
    row = lax.broadcasted_iota(jnp.int32, (16, 128), 0)
    lane = lax.broadcasted_iota(jnp.int32, (16, 128), 1)
    flags = jnp.zeros((16, 128), jnp.int32)
    for i in range(2):
        for g in range(8):
            f0, f1 = tiles[i, 2 * g], tiles[i, 2 * g + 1]

            def read(q, i=i, g=g):
                return x_ref[pl.ds(i * TILE + 16 * q, 16), pl.ds(g * 128, 128)]

            put_pair(o_ref, 0, slot, SLAB_CAP, f0, f1, read)
            slot = slot + f0 + f1
            for j, f in enumerate((f0, f1)):
                here = (row == i) & (lane == 16 + 2 * g + j)
                flags = jnp.where(here, f, flags)
    o_ref[pl.ds(64, 16), pl.ds(768, 128)] = flags.astype(jnp.float32).astype(o_ref.dtype)


def pack_slab(slab, tiles):
    return pl.pallas_call(
        pack_slab_kernel,
        in_specs=[pl.BlockSpec(memory_space=pltpu.SMEM), pl.BlockSpec(memory_space=pltpu.VMEM)],
        out_specs=pl.BlockSpec(memory_space=pltpu.VMEM),
        out_shape=jax.ShapeDtypeStruct((80, 1024), slab.dtype),
        name="pack_slab",
    )(tiles, slab)


def pack_markov_kernel(tiles, slab_tiles, flags_ref, x_ref, slab_ref, up_ref, down_ref, poison_ref):
    dtype = x_ref.dtype
    z = lax.axis_index("z")
    slab_count = 0
    for i in range(2):
        for j in range(16):
            slab_count = slab_count + slab_tiles[i, j]
    fits = slab_count <= SLAB_CAP
    for ref, sign, reach in ((up_ref, 1, 4), (down_ref, -1, 3)):
        ref[pl.ds(80, 80), :] = slab_ref[...]
        ref[pl.ds(160, 96), :] = jnp.zeros((96, 1024), dtype)

        slot = 0
        for e in range(reach):
            to = lax.rem(z + sign * (e + 1) + NZ, NZ) * 16

            def one(t, slot, ref=ref, to=to):
                f0, f1 = tiles[to + t, 0], tiles[to + t, 1]

                @pl.when(f0 + f1 > 0)
                def _():
                    def read(q):
                        return x_ref[pl.ds(pl.multiple_of((to + t) * TILE + 16 * q, 16), 16), :]

                    put_pair(ref, 160, slot, CAP, f0, f1, read)

                return slot + f0 + f1

            slot = lax.fori_loop(0, 16, one, slot, unroll=4)
        fits = fits & (slot <= CAP)
        for e in range(reach):
            to = lax.rem(z + sign * (e + 1) + NZ, NZ) * 16
            flags = flags_ref[pl.ds(pl.multiple_of(to, 16), 16), :].astype(jnp.float32).astype(dtype)
            ref[pl.ds(240, 16), pl.ds(512 + 128 * e, 2)] = flags
    poison_ref[...] = jnp.full((16, 128), jnp.where(fits, 0.0, jnp.nan), dtype)


def pack_markov(markov, markov_tiles, slab_tiles, slab):
    payload = jax.ShapeDtypeStruct((256, 1024), markov.dtype)
    return pl.pallas_call(
        pack_markov_kernel,
        in_specs=[pl.BlockSpec(memory_space=pltpu.SMEM)] * 2 + [pl.BlockSpec(memory_space=pltpu.VMEM)] * 3,
        out_specs=[pl.BlockSpec(memory_space=pltpu.VMEM)] * 3,
        out_shape=[payload, payload, jax.ShapeDtypeStruct((16, 128), markov.dtype)],
        compiler_params=pltpu.CompilerParams(vmem_limit_bytes=16 * 2**20),
        cost_estimate=pl.CostEstimate(flops=2**23, bytes_accessed=20 * 2**20, transcendentals=0),
        name="pack_markov",
    )(markov_tiles, slab_tiles, markov_tiles, markov, slab)


def own_rows_kernel(tiles, poison_ref, x_ref, o_ref, block, sem):
    dtype = x_ref.dtype
    z = lax.axis_index("z")
    copy = pltpu.make_async_copy(x_ref.at[pl.ds(pl.multiple_of(z * 1024, 1024), 1024), :], block, sem)
    copy.start()
    copy.wait()
    poison = poison_ref[pl.ds(0, 1), :]
    for i in range(16):
        rows = pl.ds(i * TILE, TILE)
        o_ref[0, rows, :] = block[rows, :] * keep(tiles[z * 16 + i, 0], tiles[z * 16 + i, 1], dtype) + poison


def own_rows(markov, markov_tiles, poison):
    return pl.pallas_call(
        own_rows_kernel,
        in_specs=[
            pl.BlockSpec(memory_space=pltpu.SMEM),
            pl.BlockSpec(memory_space=pltpu.VMEM),
            pl.BlockSpec(memory_space=pl.ANY),
        ],
        out_specs=pl.BlockSpec(memory_space=pltpu.VMEM),
        out_shape=jax.ShapeDtypeStruct((1, 1024, 128), markov.dtype),
        scratch_shapes=[pltpu.VMEM((1024, 128), markov.dtype), pltpu.SemaphoreType.DMA],
        cost_estimate=pl.CostEstimate(flops=2**20, bytes_accessed=4 * 2**20, transcendentals=0),
        name="own_rows",
    )(markov_tiles, poison, markov)


def stage_kernel(step, ref, other_ref, later, slabs_ref, token_ref, *rest):
    words, scalars, sem = rest[-3:]
    start = ref.shape[0] - 176
    groups = [ref[pl.ds(start + 160, 16), pl.ds(512 + 128 * e, 128)].astype(jnp.float32) for e in range(max(step, 1))]
    words[pl.ds(0, 16), :] = groups[-1].astype(jnp.int32)
    for k, (slab_ref, base) in enumerate(((ref, start), (other_ref, 0))):
        flags = slab_ref[pl.ds(base + 64, 16), pl.ds(768, 128)].astype(jnp.float32)
        words[pl.ds(16 + 8 * k, 8), :] = flags[:8].astype(jnp.int32)
    before = jnp.zeros((1, 128), jnp.float32)
    for flags in groups[:-1]:
        before = before + jnp.sum(flags, axis=0, keepdims=True)
    words[pl.ds(32, 8), :] = jnp.broadcast_to(before, (8, 128)).astype(jnp.int32)
    copy = pltpu.make_async_copy(words, scalars, sem)
    copy.start()
    token_ref[...] = jnp.zeros(token_ref.shape, token_ref.dtype)
    copy.wait()
    unroll = step > 2
    for h, (source, base) in enumerate(((ref, start), (other_ref, 0))):

        def four(t, slot, h=h, source=source, base=base):
            i, g0 = t // 2, 4 * (t % 2)
            flags, outs = [], []
            for g in range(4):
                word = 16 + 2 * (g0 + g)
                flags.append((scalars[16 + 8 * h + i, word], scalars[16 + 8 * h + i, word + 1]))

                def out(q, x, g=g):
                    rows = pl.ds(pl.multiple_of(i * TILE + 16 * q, 16), 16)
                    slabs_ref[0, h, rows, pl.ds(pl.multiple_of(128 * (g0 + g), 128), 128)] = x

                outs.append(out)
            return take_pairs(source, base, SLAB_CAP, slot, flags, outs)

        lax.fori_loop(0, 4, four, 0, unroll=unroll)
    if step > 0:

        def rows_of_four(t, slot):
            flags, outs = [], []
            for i in range(4):
                flags.append((scalars[4 * t + i, 0], scalars[4 * t + i, 1]))

                def out(q, x, i=i):
                    at = pl.ds(pl.multiple_of((4 * t + i) * TILE + 16 * q, 16), 16)
                    rest[0][0, at, :] = x

                outs.append(out)
            return take_pairs(ref, start + 80, CAP, slot, flags, outs)

        lax.fori_loop(0, 4, rows_of_four, scalars[32, 0] + scalars[32, 1], unroll=unroll)


def stage(step, source, other, later):
    dtype = source.dtype
    shapes = [
        jax.ShapeDtypeStruct((1, 2, 128, 1024), dtype),
        jax.ShapeDtypeStruct((16, 128), dtype),
        jax.ShapeDtypeStruct((1, 1024, 128), dtype),
    ]
    shapes = shapes if step > 0 else shapes[:2]
    return pl.pallas_call(
        functools.partial(stage_kernel, step),
        in_specs=[pl.BlockSpec(memory_space=pltpu.VMEM)] * 2 + [pl.BlockSpec(memory_space=pl.ANY)],
        out_specs=[pl.BlockSpec(memory_space=pltpu.VMEM)] * len(shapes),
        out_shape=shapes,
        scratch_shapes=[
            pltpu.VMEM((40, 128), jnp.int32),
            pltpu.SMEM((40, 128), jnp.int32),
            pltpu.SemaphoreType.DMA,
        ],
        compiler_params=pltpu.CompilerParams(vmem_limit_bytes=16 * 2**20),
        cost_estimate=pl.CostEstimate(flops=2**23, bytes_accessed=100 * 2**20, transcendentals=0),
        name="stage",
    )(source, other, later)


def encode(p):
    code = jnp.round((jnp.log2(jnp.maximum(p, 0.15)) - LOW) * (1.0 / STEP)) - 32767.0
    code = jnp.where(p > 0.0, code, jnp.where(p == 0.0, -32768.0, 32767.0))
    return code.astype(jnp.int32).astype(jnp.int16)


def decode(q):
    f = q.astype(jnp.int32).astype(jnp.float32)
    p = jnp.exp2((f + 32767.0) * STEP + LOW)
    return jnp.where(f > -32768.0, jnp.where(f < 32767.0, p, jnp.inf), 0.0)


def product_kernel(counts, part, first, last, *refs):
    n = len(counts)
    lefts, slabs = (refs[:n], refs[n : 2 * n]), refs[2 * n : 3 * n]
    earlier = None if first else refs[3 * n]
    out_ref, left, right, acc, sems, acc_sems = refs[-6:]
    width = right.shape[1]
    cols = pl.ds(part * width, width)
    same = lax.axis_index("xh") == lax.axis_index("core")
    rows = 256
    copies, accs = [], []

    def copy(src, dst):
        copies.append(pltpu.make_async_copy(src, dst, sems.at[len(copies)]))
        copies[-1].start()

    for other in range(2):
        slot = jnp.where(same, other, 1 - other)
        place = 0
        for i, count in enumerate(counts):
            for k in range(count):
                copy(lefts[other][i].at[k], left.at[:, pl.ds(place + 128 * other, 128)])
                at = pl.ds(pl.multiple_of(place + 128 * slot, 128), 128)
                copy(slabs[i].at[k, other, :, cols], right.at[at, :])
                place += 256
    if not first:
        for m in range(1024 // rows):
            at = pl.ds(m * rows, rows)
            accs.append(pltpu.make_async_copy(earlier.at[at, cols], acc.at[at, :], acc_sems.at[m]))
            accs[-1].start()
    for c in copies:
        c.wait()
    for c in accs:
        c.wait()
    step = width // 4 if first and last else width

    def block(t, _):
        m, c = t // (width // step), lax.rem(t, width // step)
        at = pl.ds(pl.multiple_of(m * rows, rows), rows)
        over = pl.ds(pl.multiple_of(c * step, step), step)
        p = jnp.dot(left[at, :], right[:, over], preferred_element_type=jnp.float32)
        if not first:
            p = p + acc[at, over]
        if last:
            q = encode(p)
            for i in range(rows // 128):
                out_ref[m * (rows // 128) + i, :, over] = q[i * 128 : (i + 1) * 128]
        else:
            out_ref[at, over] = p
        return 0

    lax.fori_loop(0, 1024 // rows * (width // step), block, 0, unroll=2 if last and not first else 1)


def product(left, other_left, right, earlier=None, part=0, parts=1, last=True):
    counts = tuple(x.shape[0] for x in left)
    n, depth, width = len(counts), 256 * sum(counts), 1024 // parts
    operands = [*left, *other_left, *right] + ([] if earlier is None else [earlier])
    if last:
        out = jax.ShapeDtypeStruct((8, 128, width), jnp.int16)
    else:
        out = jax.ShapeDtypeStruct((1024, width), jnp.float32)
    return pl.pallas_call(
        functools.partial(product_kernel, counts, part, earlier is None, last),
        in_specs=[pl.BlockSpec(memory_space=pl.ANY)] * len(operands),
        out_specs=pl.BlockSpec(memory_space=pltpu.VMEM),
        out_shape=out,
        scratch_shapes=[
            pltpu.VMEM((1024, depth), jnp.bfloat16),
            pltpu.VMEM((depth, width), jnp.bfloat16),
            pltpu.VMEM((8 if earlier is None else 1024, width), jnp.float32),
            pltpu.SemaphoreType.DMA((4 * sum(counts),)),
            pltpu.SemaphoreType.DMA((4,)),
        ],
        compiler_params=pltpu.CompilerParams(vmem_limit_bytes=20 * 2**20),
        cost_estimate=pl.CostEstimate(
            flops=2 * 1024 * depth * width, bytes_accessed=10 * 2**20, transcendentals=1024 * width
        ),
        name="product",
    )(*operands)


def square_kernel(q_ref, s_ref, sum_ref):
    def columns(t, _):
        cols = pl.ds(pl.multiple_of(t * 256, 256), 256)
        sums = jnp.zeros((16, 256), jnp.float32)
        for r in range(0, 128, 16):
            rows = pl.ds(r, 16)
            total = decode(q_ref[0, rows, cols])
            for i in range(1, 8):
                total = total + decode(q_ref[i, rows, cols])
            s = total * total
            s_ref[rows, cols] = s
            sums = sums + s
        sums = jnp.sum(sums, axis=0, keepdims=True)[None]
        sum_ref[:, :, cols] = jnp.broadcast_to(sums, (128, 1, 256))
        return 0

    lax.fori_loop(0, s_ref.shape[1] // 256, columns, 0)


def squares(q):
    width = q.shape[2]
    return pl.pallas_call(
        square_kernel,
        in_specs=[pl.BlockSpec(memory_space=pltpu.VMEM)],
        out_specs=[pl.BlockSpec(memory_space=pltpu.VMEM)] * 2,
        out_shape=[jax.ShapeDtypeStruct((128, width), jnp.float32), jax.ShapeDtypeStruct((128, 1, width), jnp.float32)],
        cost_estimate=pl.CostEstimate(flops=2**24, bytes_accessed=10 * 2**20, transcendentals=1024 * width),
        name="squares",
    )(q)


def up(x):
    return lax.ppermute(x, "z", [(i, (i + 1) % NZ) for i in range(NZ)])


def down(x):
    return lax.ppermute(x, "z", [(i, (i - 1) % NZ) for i in range(NZ)])


def across(x):
    return lax.ppermute(x, "xh", [(0, 1), (1, 0)])


def swap_core(x):
    return lax.ppermute(x, "core", [(0, 1), (1, 0)])


def exchange(left, other_left, right, earlier=None):
    parts = []
    for part in range(PARTS):
        codes = product(left, other_left, right, earlier, part, PARTS)
        parts.append(squares(lax.all_to_all(codes, ("y", "xl"), 0, 0, tiled=True)))
    sums = jnp.concatenate([b for _, b in parts], axis=2)
    return [a for a, _ in parts], jnp.sum(lax.all_to_all(sums, ALL, 0, 0, tiled=True), axis=0)


def inflate(squared, sums):
    return jnp.concatenate(squared, axis=1) / (sums / 16384.0 + 1e-06)


def dense(markov, markov_tiles, slab, slab_tiles):
    left = masked(markov, markov_tiles, 128).reshape(NZ, 1024, 128)
    left = lax.all_to_all(left, "z", 0, 0, tiled=True)
    z = lax.axis_index("z")
    own = masked(slab, slab_tiles, 128)
    own = jnp.stack([own, across(own)])

    def gather(k, carry):
        block, blocks = carry
        return down(block), lax.dynamic_update_index_in_dim(blocks, block, lax.rem(z + k, NZ), 0)

    _, right = lax.fori_loop(0, NZ, gather, (own, jnp.zeros((NZ, *own.shape), own.dtype)))
    return inflate(*exchange([left], [swap_core(left)], [right]))


def per_device(markov, markov_tiles, slab, slab_tiles):
    own = pack_slab(slab, slab_tiles)
    other = across(own)
    p, n, poison = pack_markov(markov, markov_tiles, slab_tiles, own)
    p, n = (lax.dynamic_update_slice(x, other, (0, 0)) for x in (p, n))
    lefts = [own_rows(markov, markov_tiles, poison)]
    others = [swap_core(lefts[0])]
    right, token = stage(0, p, p, lefts[0])
    rights = [right]
    for step in range(1, 5):
        if step < 4:
            p, n = up(p), down(n)
            p, n = (lax.dynamic_update_slice(x, token, (240, 256)) for x in (p, n))
            arrived = [(p, p), (n, n)]
        else:
            arrived = [(up(p[80:]), down(n[:80]))]
            token = early = product(lefts[:5], others[:5], rights[:5], last=False)
        for x, other in arrived:
            right, token, left = stage(step, x, other, token)
            lefts.append(left)
            others.append(swap_core(left))
            rights.append(right)
    squared, sums = exchange(lefts[5:], others[5:], rights[5:], early)
    return lax.cond(
        sums[0, 0] < 1e30,
        lambda: inflate(squared, sums),
        lambda: dense(markov, markov_tiles, slab, slab_tiles),
    )


def solution(mesh):
    fine = Mesh(mesh.devices.reshape(NZ, NY, NX, 2, 2), ("z", "y", "xl", "xh", "core"))
    layer = ("z", "y", "xl")
    in_specs = (
        P("xh", layer + ("core",)),
        P("xh", layer + ("core",)),
        P(layer + ("xh",), "core"),
        P(layer + ("xh",), "core"),
    )
    return jax.shard_map(
        per_device, mesh=fine, in_specs=in_specs, out_specs=P(("xh",) + layer, "core"), check_vma=False
    )
```

```python
import functools

import jax
import jax.numpy as jnp
from jax import lax
from jax.experimental import pallas as pl
from jax.experimental.pallas import tpu as pltpu
from jax.sharding import Mesh
from jax.sharding import PartitionSpec as P

NZ, NY, NX = 8, 4, 2
TILE = 64
CAP = 21
SLAB_CAP = 19
PARTS = 1
ALL = ("z", "y", "xl", "xh")
LOW = -2.75
STEP = 13.8 / 65534.0


def lanes(rows):
    return lax.broadcasted_iota(jnp.int32, (rows, 128), 1) < TILE


def mask_kernel(tiles, x_ref, o_ref):
    rows, cols = x_ref.shape
    half = lanes(TILE)
    base = pl.program_id(0) * (rows // TILE)
    for i in range(rows // TILE):
        for g in range(cols // 128):
            keep = jnp.where(half, tiles[base + i, 2 * g], tiles[base + i, 2 * g + 1])
            at = (pl.ds(i * TILE, TILE), pl.ds(g * 128, 128))
            x = x_ref[at].astype(jnp.float32)
            o_ref[at] = jnp.where(keep != 0, x, 0.0).astype(o_ref.dtype)


def masked(x, tiles, block):
    return pl.pallas_call(
        mask_kernel,
        grid=(x.shape[0] // block,),
        in_specs=[
            pl.BlockSpec(memory_space=pltpu.SMEM),
            pl.BlockSpec((block, x.shape[1]), lambda i: (i, 0)),
        ],
        out_specs=pl.BlockSpec((block, x.shape[1]), lambda i: (i, 0)),
        out_shape=jax.ShapeDtypeStruct(x.shape, x.dtype),
        name="mask",
    )(tiles, x)


def halves(x):
    return jnp.concatenate([x[:, TILE:], x[:, :TILE]], axis=1)


def half_masks(dtype):
    left = (lax.broadcasted_iota(jnp.int32, (16, 128), 1) < TILE).astype(jnp.float32)
    return left.astype(dtype), (1.0 - left).astype(dtype)


def keep(f0, f1, dtype):
    return jnp.where(lanes(TILE), f0, f1).astype(jnp.float32).astype(dtype)


def slot_parts(base, slot):
    rows = pl.ds(pl.multiple_of(base + 16 * (slot // 4), 16), 16)
    col = 256 * (slot % 4)
    return tuple((rows, pl.ds(pl.multiple_of(col + 128 * k, 128), 128)) for k in range(2))


def put_pair(ref, base, slot, cap, f0, f1, read):
    left, right = half_masks(ref.dtype)

    @pl.when((f0 > 0) & (slot < cap))
    def _():
        for k, at in enumerate(slot_parts(base, slot)):
            ref[at] = read(2 * k) * left + halves(read(2 * k + 1)) * right

    @pl.when((f1 > 0) & (slot + f0 < cap))
    def _():
        for k, at in enumerate(slot_parts(base, slot + f0)):
            ref[at] = halves(read(2 * k)) * left + read(2 * k + 1) * right


def take_pairs(ref, base, cap, slot, flags, outs):
    left, right = half_masks(ref.dtype)
    loaded = []
    for f0, f1 in flags:
        pair = []
        for f in (f0, f1):
            pair.append([ref[at] for at in slot_parts(base, jnp.minimum(slot, cap - 1))])
            slot = slot + f
        loaded.append(pair)
    for (f0, f1), (a, b), out in zip(flags, loaded, outs):
        zero = jnp.zeros((16, 128), jnp.float32)
        l = left * (zero + f0.astype(jnp.float32)).astype(ref.dtype)
        r = right * (zero + f1.astype(jnp.float32)).astype(ref.dtype)
        for k in range(2):
            out(2 * k, a[k] * l + halves(b[k]) * r)
            out(2 * k + 1, halves(a[k]) * l + b[k] * r)
    return slot


def pack_slab_kernel(tiles, x_ref, o_ref):
    o_ref[...] = jnp.zeros_like(o_ref)
    slot = 0
    row = lax.broadcasted_iota(jnp.int32, (16, 128), 0)
    lane = lax.broadcasted_iota(jnp.int32, (16, 128), 1)
    flags = jnp.zeros((16, 128), jnp.int32)
    for i in range(2):
        for g in range(8):
            f0, f1 = tiles[i, 2 * g], tiles[i, 2 * g + 1]

            def read(q, i=i, g=g):
                return x_ref[pl.ds(i * TILE + 16 * q, 16), pl.ds(g * 128, 128)]

            put_pair(o_ref, 0, slot, SLAB_CAP, f0, f1, read)
            slot = slot + f0 + f1
            for j, f in enumerate((f0, f1)):
                here = (row == i) & (lane == 16 + 2 * g + j)
                flags = jnp.where(here, f, flags)
    o_ref[pl.ds(64, 16), pl.ds(768, 128)] = flags.astype(jnp.float32).astype(o_ref.dtype)


def pack_slab(slab, tiles):
    return pl.pallas_call(
        pack_slab_kernel,
        in_specs=[pl.BlockSpec(memory_space=pltpu.SMEM), pl.BlockSpec(memory_space=pltpu.VMEM)],
        out_specs=pl.BlockSpec(memory_space=pltpu.VMEM),
        out_shape=jax.ShapeDtypeStruct((80, 1024), slab.dtype),
        name="pack_slab",
    )(tiles, slab)


def pack_markov_kernel(tiles, slab_tiles, flags_ref, x_ref, slab_ref, up_ref, down_ref, poison_ref, sems):
    dtype = x_ref.dtype
    z = lax.axis_index("z")
    slab_count = 0
    for i in range(2):
        for j in range(16):
            slab_count = slab_count + slab_tiles[i, j]
    fits = slab_count <= SLAB_CAP
    copies = [
        pltpu.make_async_copy(slab_ref, ref.at[pl.ds(80, 80), :], sems.at[k]) for k, ref in enumerate((up_ref, down_ref))
    ]
    for c in copies:
        c.start()
    for ref, sign, reach in ((up_ref, 1, 4), (down_ref, -1, 3)):
        ref[pl.ds(160, 96), :] = jnp.zeros((96, 1024), dtype)

        slot = 0
        for e in range(reach):
            to = lax.rem(z + sign * (e + 1) + NZ, NZ) * 16

            def one(t, slot, ref=ref, to=to):
                f0, f1 = tiles[to + t, 0], tiles[to + t, 1]

                @pl.when(f0 + f1 > 0)
                def _():
                    def read(q):
                        return x_ref[pl.ds(pl.multiple_of((to + t) * TILE + 16 * q, 16), 16), :]

                    put_pair(ref, 160, slot, CAP, f0, f1, read)

                return slot + f0 + f1

            slot = lax.fori_loop(0, 16, one, slot, unroll=4)
        fits = fits & (slot <= CAP)
        for e in range(reach):
            to = lax.rem(z + sign * (e + 1) + NZ, NZ) * 16
            flags = flags_ref[pl.ds(pl.multiple_of(to, 16), 16), :].astype(jnp.float32).astype(dtype)
            ref[pl.ds(240, 16), pl.ds(512 + 128 * e, 2)] = flags
    for c in copies:
        c.wait()
    poison_ref[...] = jnp.full((16, 128), jnp.where(fits, 0.0, jnp.nan), dtype)


def pack_markov(markov, markov_tiles, slab_tiles, slab):
    payload = jax.ShapeDtypeStruct((256, 1024), markov.dtype)
    return pl.pallas_call(
        pack_markov_kernel,
        in_specs=[pl.BlockSpec(memory_space=pltpu.SMEM)] * 2
        + [pl.BlockSpec(memory_space=pltpu.VMEM)] * 2
        + [pl.BlockSpec(memory_space=pl.ANY)],
        out_specs=[pl.BlockSpec(memory_space=pltpu.VMEM)] * 3,
        out_shape=[payload, payload, jax.ShapeDtypeStruct((16, 128), markov.dtype)],
        scratch_shapes=[pltpu.SemaphoreType.DMA((2,))],
        compiler_params=pltpu.CompilerParams(vmem_limit_bytes=16 * 2**20),
        cost_estimate=pl.CostEstimate(flops=2**23, bytes_accessed=20 * 2**20, transcendentals=0),
        name="pack_markov",
    )(markov_tiles, slab_tiles, markov_tiles, markov, slab)


def own_rows_kernel(tiles, poison_ref, x_ref, o_ref, block, sem):
    dtype = x_ref.dtype
    z = lax.axis_index("z")
    copy = pltpu.make_async_copy(x_ref.at[pl.ds(pl.multiple_of(z * 1024, 1024), 1024), :], block, sem)
    copy.start()
    copy.wait()
    poison = poison_ref[pl.ds(0, 1), :]
    for i in range(16):
        rows = pl.ds(i * TILE, TILE)
        o_ref[0, rows, :] = block[rows, :] * keep(tiles[z * 16 + i, 0], tiles[z * 16 + i, 1], dtype) + poison


def own_rows(markov, markov_tiles, poison):
    return pl.pallas_call(
        own_rows_kernel,
        in_specs=[
            pl.BlockSpec(memory_space=pltpu.SMEM),
            pl.BlockSpec(memory_space=pltpu.VMEM),
            pl.BlockSpec(memory_space=pl.ANY),
        ],
        out_specs=pl.BlockSpec(memory_space=pltpu.VMEM),
        out_shape=jax.ShapeDtypeStruct((1, 1024, 128), markov.dtype),
        scratch_shapes=[pltpu.VMEM((1024, 128), markov.dtype), pltpu.SemaphoreType.DMA],
        cost_estimate=pl.CostEstimate(flops=2**20, bytes_accessed=4 * 2**20, transcendentals=0),
        name="own_rows",
    )(markov_tiles, poison, markov)


def stage_kernel(step, ref, other_ref, later, slabs_ref, token_ref, *rest):
    words, scalars, sem = rest[-3:]
    start = ref.shape[0] - 176
    groups = [ref[pl.ds(start + 160, 16), pl.ds(512 + 128 * e, 128)].astype(jnp.float32) for e in range(max(step, 1))]
    words[pl.ds(0, 16), :] = groups[-1].astype(jnp.int32)
    for k, (slab_ref, base) in enumerate(((ref, start), (other_ref, 0))):
        flags = slab_ref[pl.ds(base + 64, 16), pl.ds(768, 128)].astype(jnp.float32)
        words[pl.ds(16 + 8 * k, 8), :] = flags[:8].astype(jnp.int32)
    before = jnp.zeros((1, 128), jnp.float32)
    for flags in groups[:-1]:
        before = before + jnp.sum(flags, axis=0, keepdims=True)
    words[pl.ds(32, 8), :] = jnp.broadcast_to(before, (8, 128)).astype(jnp.int32)
    copy = pltpu.make_async_copy(words, scalars, sem)
    copy.start()
    token_ref[...] = jnp.zeros(token_ref.shape, token_ref.dtype)
    copy.wait()
    unroll = step > 2 or ref.shape[0] == 176
    for h, (source, base) in enumerate(((ref, start), (other_ref, 0))):

        def four(t, slot, h=h, source=source, base=base):
            i, g0 = t // 2, 4 * (t % 2)
            flags, outs = [], []
            for g in range(4):
                word = 16 + 2 * (g0 + g)
                flags.append((scalars[16 + 8 * h + i, word], scalars[16 + 8 * h + i, word + 1]))

                def out(q, x, g=g):
                    rows = pl.ds(pl.multiple_of(i * TILE + 16 * q, 16), 16)
                    slabs_ref[0, h, rows, pl.ds(pl.multiple_of(128 * (g0 + g), 128), 128)] = x

                outs.append(out)
            return take_pairs(source, base, SLAB_CAP, slot, flags, outs)

        lax.fori_loop(0, 4, four, 0, unroll=unroll)
    if step > 0:

        def rows_of_four(t, slot):
            flags, outs = [], []
            for i in range(4):
                flags.append((scalars[4 * t + i, 0], scalars[4 * t + i, 1]))

                def out(q, x, i=i):
                    at = pl.ds(pl.multiple_of((4 * t + i) * TILE + 16 * q, 16), 16)
                    rest[0][0, at, :] = x

                outs.append(out)
            return take_pairs(ref, start + 80, CAP, slot, flags, outs)

        lax.fori_loop(0, 4, rows_of_four, scalars[32, 0] + scalars[32, 1], unroll=unroll)


def stage(step, source, other, later):
    dtype = source.dtype
    shapes = [
        jax.ShapeDtypeStruct((1, 2, 128, 1024), dtype),
        jax.ShapeDtypeStruct((16, 128), dtype),
        jax.ShapeDtypeStruct((1, 1024, 128), dtype),
    ]
    shapes = shapes if step > 0 else shapes[:2]
    return pl.pallas_call(
        functools.partial(stage_kernel, step),
        in_specs=[pl.BlockSpec(memory_space=pltpu.VMEM)] * 2 + [pl.BlockSpec(memory_space=pl.ANY)],
        out_specs=[pl.BlockSpec(memory_space=pltpu.VMEM)] * len(shapes),
        out_shape=shapes,
        scratch_shapes=[
            pltpu.VMEM((40, 128), jnp.int32),
            pltpu.SMEM((40, 128), jnp.int32),
            pltpu.SemaphoreType.DMA,
        ],
        compiler_params=pltpu.CompilerParams(vmem_limit_bytes=16 * 2**20),
        cost_estimate=pl.CostEstimate(flops=2**23, bytes_accessed=100 * 2**20, transcendentals=0),
        name="stage",
    )(source, other, later)


def last_left_kernel(step, ref, later, left_ref, words, scalars, sem):
    start = ref.shape[0] - 176
    groups = [ref[pl.ds(start + 160, 16), pl.ds(512 + 128 * e, 128)].astype(jnp.float32) for e in range(step)]
    words[pl.ds(0, 16), :] = groups[-1].astype(jnp.int32)
    before = jnp.zeros((1, 128), jnp.float32)
    for flags in groups[:-1]:
        before = before + jnp.sum(flags, axis=0, keepdims=True)
    words[pl.ds(16, 8), :] = jnp.broadcast_to(before, (8, 128)).astype(jnp.int32)
    copy = pltpu.make_async_copy(words, scalars, sem)
    copy.start()
    copy.wait()
    slot = scalars[16, 0] + scalars[16, 1]
    for t in range(4):
        flags, outs = [], []
        for i in range(4 * t, 4 * t + 4):
            flags.append((scalars[i, 0], scalars[i, 1]))

            def out(q, x, i=i):
                left_ref[0, pl.ds(i * TILE + 16 * q, 16), :] = x

            outs.append(out)
        slot = take_pairs(ref, start + 80, CAP, slot, flags, outs)


def last_left(step, source, later):
    return pl.pallas_call(
        functools.partial(last_left_kernel, step),
        in_specs=[pl.BlockSpec(memory_space=pltpu.VMEM), pl.BlockSpec(memory_space=pl.ANY)],
        out_specs=pl.BlockSpec(memory_space=pltpu.VMEM),
        out_shape=jax.ShapeDtypeStruct((1, 1024, 128), source.dtype),
        scratch_shapes=[
            pltpu.VMEM((24, 128), jnp.int32),
            pltpu.SMEM((24, 128), jnp.int32),
            pltpu.SemaphoreType.DMA,
        ],
        cost_estimate=pl.CostEstimate(flops=2**20, bytes_accessed=2 * 2**20, transcendentals=0),
        name="last_left",
    )(source, later)


def encode(p):
    code = jnp.round((jnp.log2(jnp.maximum(p, 0.15)) - LOW) * (1.0 / STEP)) - 32767.0
    code = jnp.where(p > 0.0, code, jnp.where(p == 0.0, -32768.0, 32767.0))
    return code.astype(jnp.int32).astype(jnp.int16)


def decode(q):
    f = q.astype(jnp.int32).astype(jnp.float32)
    p = jnp.exp2((f + 32767.0) * STEP + LOW)
    return jnp.where(f > -32768.0, jnp.where(f < 32767.0, p, jnp.inf), 0.0)


def product_kernel(counts, part, first, last, *refs):
    n = len(counts)
    lefts, slabs = (refs[:n], refs[n : 2 * n]), refs[2 * n : 3 * n]
    earlier = None if first else refs[3 * n]
    out_ref, left, right, acc, sems, acc_sems = refs[-6:]
    width = right.shape[1]
    cols = pl.ds(part * width, width)
    same = lax.axis_index("xh") == lax.axis_index("core")
    rows = 256
    copies, accs = [], []

    def copy(src, dst):
        copies.append(pltpu.make_async_copy(src, dst, sems.at[len(copies)]))
        copies[-1].start()

    for other in range(2):
        slot = jnp.where(same, other, 1 - other)
        place = 0
        for i, count in enumerate(counts):
            for k in range(count):
                copy(lefts[other][i].at[k], left.at[:, pl.ds(place + 128 * other, 128)])
                at = pl.ds(pl.multiple_of(place + 128 * slot, 128), 128)
                copy(slabs[i].at[k, other, :, cols], right.at[at, :])
                place += 256
    if not first:
        for m in range(1024 // rows):
            at = pl.ds(m * rows, rows)
            accs.append(pltpu.make_async_copy(earlier.at[at, cols], acc.at[at, :], acc_sems.at[m]))
            accs[-1].start()
    for c in copies:
        c.wait()
    for c in accs:
        c.wait()
    step = width // 4 if first and last else width

    def block(t, _):
        m, c = t // (width // step), lax.rem(t, width // step)
        at = pl.ds(pl.multiple_of(m * rows, rows), rows)
        over = pl.ds(pl.multiple_of(c * step, step), step)
        p = jnp.dot(left[at, :], right[:, over], preferred_element_type=jnp.float32)
        if not first:
            p = p + acc[at, over]
        if last:
            q = encode(p)
            for i in range(rows // 128):
                out_ref[m * (rows // 128) + i, :, over] = q[i * 128 : (i + 1) * 128]
        else:
            out_ref[at, over] = p
        return 0

    lax.fori_loop(0, 1024 // rows * (width // step), block, 0, unroll=2 if last and not first else 1)


def product(left, other_left, right, earlier=None, part=0, parts=1, last=True):
    counts = tuple(x.shape[0] for x in left)
    n, depth, width = len(counts), 256 * sum(counts), 1024 // parts
    operands = [*left, *other_left, *right] + ([] if earlier is None else [earlier])
    if last:
        out = jax.ShapeDtypeStruct((8, 128, width), jnp.int16)
    else:
        out = jax.ShapeDtypeStruct((1024, width), jnp.float32)
    return pl.pallas_call(
        functools.partial(product_kernel, counts, part, earlier is None, last),
        in_specs=[pl.BlockSpec(memory_space=pl.ANY)] * len(operands),
        out_specs=pl.BlockSpec(memory_space=pltpu.VMEM),
        out_shape=out,
        scratch_shapes=[
            pltpu.VMEM((1024, depth), jnp.bfloat16),
            pltpu.VMEM((depth, width), jnp.bfloat16),
            pltpu.VMEM((8 if earlier is None else 1024, width), jnp.float32),
            pltpu.SemaphoreType.DMA((4 * sum(counts),)),
            pltpu.SemaphoreType.DMA((4,)),
        ],
        compiler_params=pltpu.CompilerParams(vmem_limit_bytes=20 * 2**20),
        cost_estimate=pl.CostEstimate(
            flops=2 * 1024 * depth * width, bytes_accessed=10 * 2**20, transcendentals=1024 * width
        ),
        name="product",
    )(*operands)


def square_kernel(q_ref, s_ref, sum_ref):
    def columns(t, _):
        cols = pl.ds(pl.multiple_of(t * 256, 256), 256)
        sums = jnp.zeros((16, 256), jnp.float32)
        for r in range(0, 128, 16):
            rows = pl.ds(r, 16)
            total = decode(q_ref[0, rows, cols])
            for i in range(1, 8):
                total = total + decode(q_ref[i, rows, cols])
            s = total * total
            s_ref[rows, cols] = s
            sums = sums + s
        sums = jnp.sum(sums, axis=0, keepdims=True)[None]
        sum_ref[:, :, cols] = jnp.broadcast_to(sums, (128, 1, 256))
        return 0

    lax.fori_loop(0, s_ref.shape[1] // 256, columns, 0)


def squares(q):
    width = q.shape[2]
    return pl.pallas_call(
        square_kernel,
        in_specs=[pl.BlockSpec(memory_space=pltpu.VMEM)],
        out_specs=[pl.BlockSpec(memory_space=pltpu.VMEM)] * 2,
        out_shape=[jax.ShapeDtypeStruct((128, width), jnp.float32), jax.ShapeDtypeStruct((128, 1, width), jnp.float32)],
        cost_estimate=pl.CostEstimate(flops=2**24, bytes_accessed=10 * 2**20, transcendentals=1024 * width),
        name="squares",
    )(q)


def up(x):
    return lax.ppermute(x, "z", [(i, (i + 1) % NZ) for i in range(NZ)])


def down(x):
    return lax.ppermute(x, "z", [(i, (i - 1) % NZ) for i in range(NZ)])


def across(x):
    return lax.ppermute(x, "xh", [(0, 1), (1, 0)])


def swap_core(x):
    return lax.ppermute(x, "core", [(0, 1), (1, 0)])


def exchange(left, other_left, right, earlier=None):
    parts = []
    for part in range(PARTS):
        codes = product(left, other_left, right, earlier, part, PARTS)
        parts.append(squares(lax.all_to_all(codes, ("y", "xl"), 0, 0, tiled=True)))
    sums = jnp.concatenate([b for _, b in parts], axis=2)
    return [a for a, _ in parts], jnp.sum(lax.all_to_all(sums, ALL, 0, 0, tiled=True), axis=0)


def inflate(squared, sums):
    return jnp.concatenate(squared, axis=1) / (sums / 16384.0 + 1e-06)


def dense(markov, markov_tiles, slab, slab_tiles):
    left = masked(markov, markov_tiles, 128).reshape(NZ, 1024, 128)
    left = lax.all_to_all(left, "z", 0, 0, tiled=True)
    z = lax.axis_index("z")
    own = masked(slab, slab_tiles, 128)
    own = jnp.stack([own, across(own)])

    def gather(k, carry):
        block, blocks = carry
        return down(block), lax.dynamic_update_index_in_dim(blocks, block, lax.rem(z + k, NZ), 0)

    _, right = lax.fori_loop(0, NZ, gather, (own, jnp.zeros((NZ, *own.shape), own.dtype)))
    return inflate(*exchange([left], [swap_core(left)], [right]))


def per_device(markov, markov_tiles, slab, slab_tiles):
    own = pack_slab(slab, slab_tiles)
    other = across(own)
    p, n, poison = pack_markov(markov, markov_tiles, slab_tiles, own)
    p, n = (lax.dynamic_update_slice(x, other, (0, 0)) for x in (p, n))
    lefts = [own_rows(markov, markov_tiles, poison)]
    others = [swap_core(lefts[0])]
    right, token = stage(0, p, p, lefts[0])
    rights = [right]
    for step in range(1, 5):
        if step < 4:
            p, n = up(p), down(n)
            p, n = (lax.dynamic_update_slice(x, token, (240, 256)) for x in (p, n))
            arrived = [(p, p), (n, n)]
        else:
            arrived = [(up(p[80:]), down(n[:80]))]
            token = early = product(lefts[:5], others[:5], rights[:5], last=False)
        for x, other in arrived:
            if step < 4:
                right, token, left = stage(step, x, other, token)
            else:
                left = last_left(step, x, token)
                right, token = stage(0, x, other, left)
            lefts.append(left)
            others.append(swap_core(left))
            rights.append(right)
    squared, sums = exchange(lefts[5:], others[5:], rights[5:], early)
    return lax.cond(
        sums[0, 0] < 1e30,
        lambda: inflate(squared, sums),
        lambda: dense(markov, markov_tiles, slab, slab_tiles),
    )


def solution(mesh):
    fine = Mesh(mesh.devices.reshape(NZ, NY, NX, 2, 2), ("z", "y", "xl", "xh", "core"))
    layer = ("z", "y", "xl")
    in_specs = (
        P("xh", layer + ("core",)),
        P("xh", layer + ("core",)),
        P(layer + ("xh",), "core"),
        P(layer + ("xh",), "core"),
    )
    return jax.shard_map(
        per_device, mesh=fine, in_specs=in_specs, out_specs=P(("xh",) + layer, "core"), check_vma=False
    )
```

```python
import functools

import jax
import jax.numpy as jnp
from jax import lax
from jax.experimental import pallas as pl
from jax.experimental.pallas import tpu as pltpu
from jax.sharding import Mesh
from jax.sharding import PartitionSpec as P

NZ, NY, NX = 8, 4, 2
TILE = 64
CAP = 21
SLAB_CAP = 19
PARTS = 1
LAYER = ("z", "y", "xl")
LOW = -2.75
STEP = 13.8 / 65534.0


def lanes(rows):
    return lax.broadcasted_iota(jnp.int32, (rows, 128), 1) < TILE


def mask_kernel(tiles, x_ref, o_ref):
    rows, cols = x_ref.shape
    half = lanes(TILE)
    base = pl.program_id(0) * (rows // TILE)
    for i in range(rows // TILE):
        for g in range(cols // 128):
            keep = jnp.where(half, tiles[base + i, 2 * g], tiles[base + i, 2 * g + 1])
            at = (pl.ds(i * TILE, TILE), pl.ds(g * 128, 128))
            x = x_ref[at].astype(jnp.float32)
            o_ref[at] = jnp.where(keep != 0, x, 0.0).astype(o_ref.dtype)


def masked(x, tiles, block):
    return pl.pallas_call(
        mask_kernel,
        grid=(x.shape[0] // block,),
        in_specs=[
            pl.BlockSpec(memory_space=pltpu.SMEM),
            pl.BlockSpec((block, x.shape[1]), lambda i: (i, 0)),
        ],
        out_specs=pl.BlockSpec((block, x.shape[1]), lambda i: (i, 0)),
        out_shape=jax.ShapeDtypeStruct(x.shape, x.dtype),
        name="mask",
    )(tiles, x)


def halves(x):
    return jnp.concatenate([x[:, TILE:], x[:, :TILE]], axis=1)


def half_masks(dtype):
    left = (lax.broadcasted_iota(jnp.int32, (16, 128), 1) < TILE).astype(jnp.float32)
    return left.astype(dtype), (1.0 - left).astype(dtype)


def keep(f0, f1, dtype):
    return jnp.where(lanes(TILE), f0, f1).astype(jnp.float32).astype(dtype)


def slot_parts(base, slot):
    rows = pl.ds(pl.multiple_of(base + 16 * (slot // 4), 16), 16)
    col = 256 * (slot % 4)
    return tuple((rows, pl.ds(pl.multiple_of(col + 128 * k, 128), 128)) for k in range(2))


def put_pair(ref, base, slot, cap, f0, f1, read):
    left, right = half_masks(ref.dtype)

    @pl.when((f0 > 0) & (slot < cap))
    def _():
        for k, at in enumerate(slot_parts(base, slot)):
            ref[at] = read(2 * k) * left + halves(read(2 * k + 1)) * right

    @pl.when((f1 > 0) & (slot + f0 < cap))
    def _():
        for k, at in enumerate(slot_parts(base, slot + f0)):
            ref[at] = halves(read(2 * k)) * left + read(2 * k + 1) * right


def take_pairs(ref, base, cap, slot, flags, outs):
    left, right = half_masks(ref.dtype)
    loaded = []
    for f0, f1 in flags:
        pair = []
        for f in (f0, f1):
            pair.append([ref[at] for at in slot_parts(base, jnp.minimum(slot, cap - 1))])
            slot = slot + f
        loaded.append(pair)
    for (f0, f1), (a, b), out in zip(flags, loaded, outs):
        zero = jnp.zeros((16, 128), jnp.float32)
        l = left * (zero + f0.astype(jnp.float32)).astype(ref.dtype)
        r = right * (zero + f1.astype(jnp.float32)).astype(ref.dtype)
        for k in range(2):
            out(2 * k, a[k] * l + halves(b[k]) * r)
            out(2 * k + 1, halves(a[k]) * l + b[k] * r)
    return slot


def pack_slab_kernel(tiles, x_ref, o_ref):
    o_ref[...] = jnp.zeros_like(o_ref)
    slot = 0
    row = lax.broadcasted_iota(jnp.int32, (16, 128), 0)
    lane = lax.broadcasted_iota(jnp.int32, (16, 128), 1)
    flags = jnp.zeros((16, 128), jnp.int32)
    for i in range(2):
        for g in range(8):
            f0, f1 = tiles[i, 2 * g], tiles[i, 2 * g + 1]

            def read(q, i=i, g=g):
                return x_ref[pl.ds(i * TILE + 16 * q, 16), pl.ds(g * 128, 128)]

            put_pair(o_ref, 0, slot, SLAB_CAP, f0, f1, read)
            slot = slot + f0 + f1
            for j, f in enumerate((f0, f1)):
                here = (row == i) & (lane == 16 + 2 * g + j)
                flags = jnp.where(here, f, flags)
    o_ref[pl.ds(64, 16), pl.ds(768, 128)] = flags.astype(jnp.float32).astype(o_ref.dtype)


def pack_slab(slab, tiles):
    return pl.pallas_call(
        pack_slab_kernel,
        in_specs=[pl.BlockSpec(memory_space=pltpu.SMEM), pl.BlockSpec(memory_space=pltpu.VMEM)],
        out_specs=pl.BlockSpec(memory_space=pltpu.VMEM),
        out_shape=jax.ShapeDtypeStruct((80, 1024), slab.dtype),
        name="pack_slab",
    )(tiles, slab)


def pack_markov_kernel(tiles, slab_tiles, flags_ref, x_ref, slab_ref, up_ref, down_ref, poison_ref):
    dtype = x_ref.dtype
    z = lax.axis_index("z")
    slab_count = 0
    for i in range(2):
        for j in range(16):
            slab_count = slab_count + slab_tiles[i, j]
    fits = slab_count <= SLAB_CAP
    for ref, sign, reach in ((up_ref, 1, 4), (down_ref, -1, 3)):
        ref[pl.ds(80, 80), :] = slab_ref[...]
        ref[pl.ds(160, 96), :] = jnp.zeros((96, 1024), dtype)

        slot = 0
        for e in range(reach):
            to = lax.rem(z + sign * (e + 1) + NZ, NZ) * 16

            def one(t, slot, ref=ref, to=to):
                f0, f1 = tiles[to + t, 0], tiles[to + t, 1]

                @pl.when(f0 + f1 > 0)
                def _():
                    def read(q):
                        return x_ref[pl.ds(pl.multiple_of((to + t) * TILE + 16 * q, 16), 16), :]

                    put_pair(ref, 160, slot, CAP, f0, f1, read)

                return slot + f0 + f1

            slot = lax.fori_loop(0, 16, one, slot, unroll=4)
        fits = fits & (slot <= CAP)
        for e in range(reach):
            to = lax.rem(z + sign * (e + 1) + NZ, NZ) * 16
            flags = flags_ref[pl.ds(pl.multiple_of(to, 16), 16), :].astype(jnp.float32).astype(dtype)
            ref[pl.ds(240, 16), pl.ds(512 + 128 * e, 2)] = flags
    poison_ref[...] = jnp.full((16, 128), jnp.where(fits, 0.0, jnp.nan), dtype)


def pack_markov(markov, markov_tiles, slab_tiles, slab):
    payload = jax.ShapeDtypeStruct((256, 1024), markov.dtype)
    return pl.pallas_call(
        pack_markov_kernel,
        in_specs=[pl.BlockSpec(memory_space=pltpu.SMEM)] * 2 + [pl.BlockSpec(memory_space=pltpu.VMEM)] * 3,
        out_specs=[pl.BlockSpec(memory_space=pltpu.VMEM)] * 3,
        out_shape=[payload, payload, jax.ShapeDtypeStruct((16, 128), markov.dtype)],
        compiler_params=pltpu.CompilerParams(vmem_limit_bytes=16 * 2**20),
        cost_estimate=pl.CostEstimate(flops=2**23, bytes_accessed=20 * 2**20, transcendentals=0),
        name="pack_markov",
    )(markov_tiles, slab_tiles, markov_tiles, markov, slab)


def own_rows_kernel(tiles, poison_ref, x_ref, o_ref, block, sem):
    dtype = x_ref.dtype
    z = lax.axis_index("z")
    copy = pltpu.make_async_copy(x_ref.at[pl.ds(pl.multiple_of(z * 1024, 1024), 1024), :], block, sem)
    copy.start()
    copy.wait()
    poison = poison_ref[pl.ds(0, 1), :]
    for i in range(16):
        rows = pl.ds(i * TILE, TILE)
        o_ref[0, rows, :] = block[rows, :] * keep(tiles[z * 16 + i, 0], tiles[z * 16 + i, 1], dtype) + poison


def own_rows(markov, markov_tiles, poison):
    return pl.pallas_call(
        own_rows_kernel,
        in_specs=[
            pl.BlockSpec(memory_space=pltpu.SMEM),
            pl.BlockSpec(memory_space=pltpu.VMEM),
            pl.BlockSpec(memory_space=pl.ANY),
        ],
        out_specs=pl.BlockSpec(memory_space=pltpu.VMEM),
        out_shape=jax.ShapeDtypeStruct((1, 1024, 128), markov.dtype),
        scratch_shapes=[pltpu.VMEM((1024, 128), markov.dtype), pltpu.SemaphoreType.DMA],
        cost_estimate=pl.CostEstimate(flops=2**20, bytes_accessed=4 * 2**20, transcendentals=0),
        name="own_rows",
    )(markov_tiles, poison, markov)


def stage_kernel(step, ref, other_ref, later, slabs_ref, token_ref, *rest):
    words, scalars, sem = rest[-3:]
    start = ref.shape[0] - 176
    groups = [ref[pl.ds(start + 160, 16), pl.ds(512 + 128 * e, 128)].astype(jnp.float32) for e in range(max(step, 1))]
    words[pl.ds(0, 16), :] = groups[-1].astype(jnp.int32)
    for k, (slab_ref, base) in enumerate(((ref, start), (other_ref, 0))):
        flags = slab_ref[pl.ds(base + 64, 16), pl.ds(768, 128)].astype(jnp.float32)
        words[pl.ds(16 + 8 * k, 8), :] = flags[:8].astype(jnp.int32)
    before = jnp.zeros((1, 128), jnp.float32)
    for flags in groups[:-1]:
        before = before + jnp.sum(flags, axis=0, keepdims=True)
    words[pl.ds(32, 8), :] = jnp.broadcast_to(before, (8, 128)).astype(jnp.int32)
    copy = pltpu.make_async_copy(words, scalars, sem)
    copy.start()
    token_ref[...] = jnp.zeros(token_ref.shape, token_ref.dtype)
    copy.wait()
    unroll = step > 2
    for h, (source, base) in enumerate(((ref, start), (other_ref, 0))):

        def four(t, slot, h=h, source=source, base=base):
            i, g0 = t // 2, 4 * (t % 2)
            flags, outs = [], []
            for g in range(4):
                word = 16 + 2 * (g0 + g)
                flags.append((scalars[16 + 8 * h + i, word], scalars[16 + 8 * h + i, word + 1]))

                def out(q, x, g=g):
                    rows = pl.ds(pl.multiple_of(i * TILE + 16 * q, 16), 16)
                    slabs_ref[0, h, rows, pl.ds(pl.multiple_of(128 * (g0 + g), 128), 128)] = x

                outs.append(out)
            return take_pairs(source, base, SLAB_CAP, slot, flags, outs)

        lax.fori_loop(0, 4, four, 0, unroll=unroll)
    if step > 0:

        def rows_of_four(t, slot):
            flags, outs = [], []
            for i in range(4):
                flags.append((scalars[4 * t + i, 0], scalars[4 * t + i, 1]))

                def out(q, x, i=i):
                    at = pl.ds(pl.multiple_of((4 * t + i) * TILE + 16 * q, 16), 16)
                    rest[0][0, at, :] = x

                outs.append(out)
            return take_pairs(ref, start + 80, CAP, slot, flags, outs)

        lax.fori_loop(0, 4, rows_of_four, scalars[32, 0] + scalars[32, 1], unroll=unroll)


def stage(step, source, other, later):
    dtype = source.dtype
    shapes = [
        jax.ShapeDtypeStruct((1, 2, 128, 1024), dtype),
        jax.ShapeDtypeStruct((16, 128), dtype),
        jax.ShapeDtypeStruct((1, 1024, 128), dtype),
    ]
    shapes = shapes if step > 0 else shapes[:2]
    return pl.pallas_call(
        functools.partial(stage_kernel, step),
        in_specs=[pl.BlockSpec(memory_space=pltpu.VMEM)] * 2 + [pl.BlockSpec(memory_space=pl.ANY)],
        out_specs=[pl.BlockSpec(memory_space=pltpu.VMEM)] * len(shapes),
        out_shape=shapes,
        scratch_shapes=[
            pltpu.VMEM((40, 128), jnp.int32),
            pltpu.SMEM((40, 128), jnp.int32),
            pltpu.SemaphoreType.DMA,
        ],
        compiler_params=pltpu.CompilerParams(vmem_limit_bytes=16 * 2**20),
        cost_estimate=pl.CostEstimate(flops=2**23, bytes_accessed=100 * 2**20, transcendentals=0),
        name="stage",
    )(source, other, later)


def encode(p):
    code = jnp.round((jnp.log2(jnp.maximum(p, 0.15)) - LOW) * (1.0 / STEP)) - 32767.0
    code = jnp.where(p > 0.0, code, jnp.where(p == 0.0, -32768.0, 32767.0))
    return code.astype(jnp.int32).astype(jnp.int16)


def decode(q):
    f = q.astype(jnp.int32).astype(jnp.float32)
    p = jnp.exp2((f + 32767.0) * STEP + LOW)
    return jnp.where(f > -32768.0, jnp.where(f < 32767.0, p, jnp.inf), 0.0)


def product_kernel(counts, part, first, last, *refs):
    n = len(counts)
    lefts, slabs = (refs[:n], refs[n : 2 * n]), refs[2 * n : 3 * n]
    earlier = None if first else refs[3 * n]
    out_ref, left, right, acc, sems, acc_sems = refs[-6:]
    width = right.shape[1]
    cols = pl.ds(part * width, width)
    same = lax.axis_index("xh") == lax.axis_index("core")
    rows = 256
    copies, accs = [], []

    def copy(src, dst):
        copies.append(pltpu.make_async_copy(src, dst, sems.at[len(copies)]))
        copies[-1].start()

    for other in range(2):
        slot = jnp.where(same, other, 1 - other)
        place = 0
        for i, count in enumerate(counts):
            for k in range(count):
                copy(lefts[other][i].at[k], left.at[:, pl.ds(place + 128 * other, 128)])
                at = pl.ds(pl.multiple_of(place + 128 * slot, 128), 128)
                copy(slabs[i].at[k, other, :, cols], right.at[at, :])
                place += 256
    if not first:
        for m in range(1024 // rows):
            at = pl.ds(m * rows, rows)
            accs.append(pltpu.make_async_copy(earlier.at[at, cols], acc.at[at, :], acc_sems.at[m]))
            accs[-1].start()
    for c in copies:
        c.wait()
    for c in accs:
        c.wait()
    step = width // 4 if first and last else width

    def block(t, _):
        m, c = t // (width // step), lax.rem(t, width // step)
        at = pl.ds(pl.multiple_of(m * rows, rows), rows)
        over = pl.ds(pl.multiple_of(c * step, step), step)
        p = jnp.dot(left[at, :], right[:, over], preferred_element_type=jnp.float32)
        if not first:
            p = p + acc[at, over]
        if last:
            q = encode(p)
            for i in range(rows // 128):
                out_ref[m * (rows // 128) + i, :, over] = q[i * 128 : (i + 1) * 128]
        else:
            out_ref[at, over] = p
        return 0

    lax.fori_loop(0, 1024 // rows * (width // step), block, 0, unroll=2 if last and not first else 1)


def product(left, other_left, right, earlier=None, part=0, parts=1, last=True):
    counts = tuple(x.shape[0] for x in left)
    n, depth, width = len(counts), 256 * sum(counts), 1024 // parts
    operands = [*left, *other_left, *right] + ([] if earlier is None else [earlier])
    if last:
        out = jax.ShapeDtypeStruct((8, 128, width), jnp.int16)
    else:
        out = jax.ShapeDtypeStruct((1024, width), jnp.float32)
    return pl.pallas_call(
        functools.partial(product_kernel, counts, part, earlier is None, last),
        in_specs=[pl.BlockSpec(memory_space=pl.ANY)] * len(operands),
        out_specs=pl.BlockSpec(memory_space=pltpu.VMEM),
        out_shape=out,
        scratch_shapes=[
            pltpu.VMEM((1024, depth), jnp.bfloat16),
            pltpu.VMEM((depth, width), jnp.bfloat16),
            pltpu.VMEM((8 if earlier is None else 1024, width), jnp.float32),
            pltpu.SemaphoreType.DMA((4 * sum(counts),)),
            pltpu.SemaphoreType.DMA((4,)),
        ],
        compiler_params=pltpu.CompilerParams(vmem_limit_bytes=20 * 2**20),
        cost_estimate=pl.CostEstimate(
            flops=2 * 1024 * depth * width, bytes_accessed=10 * 2**20, transcendentals=1024 * width
        ),
        name="product",
    )(*operands)


def square_kernel(q_ref, s_ref, sum_ref):
    def columns(t, _):
        cols = pl.ds(pl.multiple_of(t * 256, 256), 256)
        sums = jnp.zeros((16, 256), jnp.float32)
        for r in range(0, 128, 16):
            rows = pl.ds(r, 16)
            total = decode(q_ref[0, rows, cols])
            for i in range(1, 8):
                total = total + decode(q_ref[i, rows, cols])
            s = total * total
            s_ref[rows, cols] = s
            sums = sums + s
        sums = jnp.sum(sums, axis=0, keepdims=True)[None]
        sum_ref[:, :, cols] = sums
        return 0

    lax.fori_loop(0, s_ref.shape[1] // 256, columns, 0)


def squares(q):
    width = q.shape[2]
    return pl.pallas_call(
        square_kernel,
        in_specs=[pl.BlockSpec(memory_space=pltpu.VMEM)],
        out_specs=[pl.BlockSpec(memory_space=pltpu.VMEM)] * 2,
        out_shape=[jax.ShapeDtypeStruct((128, width), jnp.float32), jax.ShapeDtypeStruct((1, 1, width), jnp.float32)],
        cost_estimate=pl.CostEstimate(flops=2**24, bytes_accessed=10 * 2**20, transcendentals=1024 * width),
        name="squares",
    )(q)


def up(x):
    return lax.ppermute(x, "z", [(i, (i + 1) % NZ) for i in range(NZ)])


def down(x):
    return lax.ppermute(x, "z", [(i, (i - 1) % NZ) for i in range(NZ)])


def across(x):
    return lax.ppermute(x, "xh", [(0, 1), (1, 0)])


def swap_core(x):
    return lax.ppermute(x, "core", [(0, 1), (1, 0)])


def exchange(left, other_left, right, earlier=None):
    parts = []
    for part in range(PARTS):
        codes = product(left, other_left, right, earlier, part, PARTS)
        parts.append(squares(lax.all_to_all(codes, ("y", "xl"), 0, 0, tiled=True)))
    sums = jnp.concatenate([b for _, b in parts], axis=2)
    sums = jnp.broadcast_to(sums + across(sums), (64, 1, 1024))
    return [a for a, _ in parts], jnp.sum(lax.all_to_all(sums, LAYER, 0, 0, tiled=True), axis=0)


def inflate(squared, sums):
    return jnp.concatenate(squared, axis=1) / (sums / 16384.0 + 1e-06)


def dense(markov, markov_tiles, slab, slab_tiles):
    left = masked(markov, markov_tiles, 128).reshape(NZ, 1024, 128)
    left = lax.all_to_all(left, "z", 0, 0, tiled=True)
    z = lax.axis_index("z")
    own = masked(slab, slab_tiles, 128)
    own = jnp.stack([own, across(own)])

    def gather(k, carry):
        block, blocks = carry
        return down(block), lax.dynamic_update_index_in_dim(blocks, block, lax.rem(z + k, NZ), 0)

    _, right = lax.fori_loop(0, NZ, gather, (own, jnp.zeros((NZ, *own.shape), own.dtype)))
    return inflate(*exchange([left], [swap_core(left)], [right]))


def per_device(markov, markov_tiles, slab, slab_tiles):
    own = pack_slab(slab, slab_tiles)
    other = across(own)
    p, n, poison = pack_markov(markov, markov_tiles, slab_tiles, own)
    p, n = (lax.dynamic_update_slice(x, other, (0, 0)) for x in (p, n))
    lefts = [own_rows(markov, markov_tiles, poison)]
    others = [swap_core(lefts[0])]
    right, token = stage(0, p, p, lefts[0])
    rights = [right]
    for step in range(1, 5):
        if step < 4:
            p, n = up(p), down(n)
            p, n = (lax.dynamic_update_slice(x, token, (240, 256)) for x in (p, n))
            arrived = [(p, p), (n, n)]
        else:
            arrived = [(up(p[80:]), down(n[:80]))]
            token = early = product(lefts[:5], others[:5], rights[:5], last=False)
        for x, other in arrived:
            right, token, left = stage(step, x, other, token)
            lefts.append(left)
            others.append(swap_core(left))
            rights.append(right)
    squared, sums = exchange(lefts[5:], others[5:], rights[5:], early)
    return lax.cond(
        sums[0, 0] < 1e30,
        lambda: inflate(squared, sums),
        lambda: dense(markov, markov_tiles, slab, slab_tiles),
    )


def solution(mesh):
    fine = Mesh(mesh.devices.reshape(NZ, NY, NX, 2, 2), ("z", "y", "xl", "xh", "core"))
    layer = ("z", "y", "xl")
    in_specs = (
        P("xh", layer + ("core",)),
        P("xh", layer + ("core",)),
        P(layer + ("xh",), "core"),
        P(layer + ("xh",), "core"),
    )
    return jax.shard_map(
        per_device, mesh=fine, in_specs=in_specs, out_specs=P(("xh",) + layer, "core"), check_vma=False
    )
```
